32 devices in a mesh: seq: 16 (over z, y, x), head: 2 (over core).
Axes of the slice: x: 2, y: 2, z: 4, core: 2. Of those that a mesh axis runs over, the one named last changes fastest.
Arguments:
- query_one: bfloat16 [2048, 32, 128], P('seq', 'head'), may hold values from -6 to 6
- key_one: bfloat16 [2048, 32, 128], P('seq', 'head'), may hold values from -6 to 6
- value_one: bfloat16 [2048, 32, 128], P('seq', 'head'), may hold values from -160 to 160
- log_decay: float32 [32, 2048], P('head', 'seq'), may hold values from -1 to 0
- query_two: bfloat16 [2048, 32, 128], P('seq', 'head'), may hold values from -24 to 24
- key_two: bfloat16 [2048, 32, 128], P('seq', 'head'), may hold values from -24 to 24
- out_grad: bfloat16 [2048, 32, 128], P('seq', 'head'), may hold values from -6 to 6
- doc_ids: int32 [16], replicated, may hold values from 0 to 3, never falling along the last dimension, each value on 1 to 8 neighbouring positions
Outputs:
- grad_query_one: float32 [2048, 32, 128], P('seq', 'head')
- grad_key_one: float32 [2048, 32, 128], P('seq', 'head')
- grad_value_one: float32 [2048, 32, 128], P('seq', 'head')
- grad_query_two: float32 [2048, 32, 128], P('seq', 'head')
- grad_key_two: float32 [2048, 32, 128], P('seq', 'head')
The draws below stay inside these ranges and needn't reach their ends.
Inputs may be any that keep to these rules, and one draw needn't show every extreme that they name: doc_ids never fall along the sequence; one document covers at most 8 blocks.
All inputs are finite; a program needn't handle non-finite values.
Results may differ from the reference program's by a relative error of at most 0.0096.
Values may be sent and summed in bfloat16 or wider, within the bound.
No kernel may reach another device: no remote copies, remote signals or barrier semaphores. Data moves between devices by JAX's collectives and lax.ppermute only.
A program may use at most 128 MiB of HBM per device.

```python
import math
import jax
import jax.numpy as jnp
import numpy as np
from jax import lax

HEADS = 32
HEAD_DIM = 128
BLOCK = 128
BLK_DEV = 1
REACH = 8
SEQUENCE_LENGTH = 2048
NBLK = 16
DOC_BLOCKS = 8
DOCS = 4


def draw_query_two(key, part):
    noise_key = jax.random.fold_in(key, 11)
    field = jnp.clip(jax.random.normal(noise_key, (SEQUENCE_LENGTH, HEADS, HEAD_DIM), jnp.float32), -6.0, 6.0)
    return field.astype(jnp.bfloat16)


def draw_key_two(key, part):
    noise_key = jax.random.fold_in(key, 13)
    field = jnp.clip(jax.random.normal(noise_key, (SEQUENCE_LENGTH, HEADS, HEAD_DIM), jnp.float32), -6.0, 6.0)
    return field.astype(jnp.bfloat16)


def draw_value_one(key, part):
    noise_key, row_key, column_key = jax.random.split(jax.random.fold_in(key, 21), 3)
    heads_share = jnp.arange(HEADS, dtype=jnp.float32) / max(HEADS - 1, 1)
    noise = jnp.clip(jax.random.normal(noise_key, (SEQUENCE_LENGTH, HEADS, HEAD_DIM), jnp.float32), -4.0, 4.0)
    rising = 3.0 ** heads_share
    row_scale = jnp.exp(jax.random.uniform(row_key, (SEQUENCE_LENGTH, 1, 1), jnp.float32, -1.15, 1.15))
    column_scale = jnp.exp(jax.random.uniform(column_key, (1, HEADS, HEAD_DIM), jnp.float32, -1.15, 1.15))
    return (noise * row_scale * column_scale * rising[None, :, None]).astype(jnp.bfloat16)


def draw_log_decay(key, part):
    every_key = jax.random.split(jax.random.fold_in(key, 31), 7)
    order = jax.random.permutation(every_key[0], HEADS)
    fast_count = HEADS // 2
    fast_heads = order < fast_count
    fast_rate = jnp.exp(jax.random.uniform(every_key[1], (HEADS,), jnp.float32, math.log(1.0 / 50.0), math.log(1.0 / 30.0)))
    slow_rate = jnp.exp(jax.random.uniform(every_key[2], (HEADS,), jnp.float32, math.log(0.05), math.log(0.3))) * (math.log(10.0) / SEQUENCE_LENGTH)
    rate = jnp.where(fast_heads, fast_rate, slow_rate)
    block_factor = jnp.exp(jax.random.uniform(every_key[3], (HEADS, NBLK), jnp.float32, -0.7, 0.7))
    roughness = jnp.exp(jax.random.uniform(every_key[4], (HEADS, SEQUENCE_LENGTH), jnp.float32, -0.35, 0.35))
    position_values = rate[:, None] * jnp.repeat(block_factor, BLOCK, axis=1) * roughness
    segment_start = jax.random.randint(every_key[5], (2,), 0, SEQUENCE_LENGTH)
    segment_length = jax.random.uniform(every_key[6], (2,), jnp.float32, math.log(0.5), math.log(0.8))
    token_position = jnp.arange(SEQUENCE_LENGTH)
    segment_list = jnp.where(token_position == segment_start[0], segment_length[0], 0.0) + jnp.where(token_position == segment_start[1], segment_length[1], 0.0)
    return (segment_list[None, :] - position_values).astype(jnp.float32)


def block_levels(rng, dims, cuts, smallest, largest):
    def one(position, parts):
        draws = jax.random.uniform(jax.random.fold_in(jax.random.fold_in(rng, 6), position), (parts,), jnp.float32, smallest / len(cuts), largest / len(cuts))
        return jnp.repeat(jnp.exp(draws), dims[position] // parts).reshape((-1,) + (1,) * (len(dims) - position - 1))

    level = one(*cuts[0])
    for cut in cuts[1:]:
        level = level * one(*cut)
    return level


def length_profile(count, total, bound, lean):
    weights = [(1 << 20) // math.isqrt(standing ** lean) + 1 for standing in range(2, count + 1)]
    spare, holding = total - bound - (count - 1), [1] * (count - 1)
    while spare > 0:
        free = [i for i in range(count - 1) if holding[i] < bound]
        whole, left = sum([weights[i] for i in free]), spare
        for i in free:
            more = min(bound - holding[i], max(1, left * weights[i] // whole), spare)
            holding[i] = holding[i] + more
            spare = spare - more
    return np.array([bound] + holding)


def uneven(stream_key, number_of, total, reach, skew):
    if number_of == 2:
        one = jax.random.randint(stream_key, (), max(1, total - reach), min(reach, total - 1) + 1)
        return jnp.stack([one, total - one])
    lengths = jnp.asarray(length_profile(number_of, total, reach, skew), jnp.int32)
    twos = (number_of - 1) // 2
    donor, taker = lengths[1:1 + 2 * twos:2], lengths[2:2 + 2 * twos:2]
    room = jnp.minimum(donor - 1, reach - taker)
    passed = jax.random.randint(jax.random.fold_in(stream_key, 1), (twos,), 0, 1 << 20) % (room + 1)
    lengths = lengths.at[1:1 + 2 * twos:2].set(donor - passed).at[2:2 + 2 * twos:2].set(taker + passed)
    return lengths[jax.random.permutation(jax.random.fold_in(stream_key, 2), number_of)]


def centred(key, dims, width, most, cuts=(), kind=jnp.bfloat16):
    result = width * jax.random.normal(key, dims, jnp.float32)
    if cuts:
        result = result * block_levels(key, dims, cuts, -0.22, 0.18)
    return jnp.clip(result, -most, most).astype(kind)


def setup_inputs(seed: int = 0) -> dict:
    key_of = jax.random.split(jax.random.key(seed), 9)
    query_one = centred(key_of[0], (SEQUENCE_LENGTH, HEADS, HEAD_DIM), 1.0, 6.0, ((0, 16), (1, 2)))
    key_one = centred(key_of[1], (SEQUENCE_LENGTH, HEADS, HEAD_DIM), 1.0, 6.0, ((0, 16), (1, 2)))
    value_one = draw_value_one(jax.random.fold_in(key_of[8], 71), 0)
    log_decay = draw_log_decay(jax.random.fold_in(key_of[8], 71), 0)
    query_two = draw_query_two(jax.random.fold_in(key_of[8], 71), 0)
    key_two = draw_key_two(jax.random.fold_in(key_of[8], 71), 0)
    out_grad = centred(key_of[6], (SEQUENCE_LENGTH, HEADS, HEAD_DIM), 1.0, 6.0, ((0, 16), (1, 2)))
    doc_ids = jnp.searchsorted(jnp.cumsum(uneven(key_of[7], DOCS, NBLK, DOC_BLOCKS, 1)), jnp.arange(NBLK), side="right").astype(jnp.int32)
    return dict(query_one=query_one, key_one=key_one, value_one=value_one, log_decay=log_decay, query_two=query_two, key_two=key_two, out_grad=out_grad, doc_ids=doc_ids)


exact_precision = lax.Precision.HIGHEST
floor_score = -1e+30
norm_epsilon = 1e-05

def lower_mask(length):
    return lax.broadcasted_iota(jnp.int32, (length, length), 0) >= lax.broadcasted_iota(jnp.int32, (length, length), 1)

def shard_output(q_float, k_float, v_float, cumulative, incoming):
    lower = lower_mask(q_float.shape[0])[None]
    gaps = cumulative[:, :, None] - cumulative[:, None, :]
    weights = jnp.where(lower, jnp.exp(jnp.where(lower, gaps, 0.0)), 0.0)
    scores = jnp.einsum('thd,uhd->htu', q_float, k_float, precision=exact_precision) * weights
    inner_part = jnp.einsum('htu,uhe->the', scores, v_float, precision=exact_precision)
    outer_part = jnp.einsum('thd,hde->the', q_float * jnp.exp(cumulative).T[:, :, None], incoming, precision=exact_precision)
    return inner_part + outer_part

def shard_state(k_float, v_float, cumulative):
    tail_decay = jnp.exp(cumulative[:, -1:] - cumulative)
    return jnp.einsum('uhd,uhe->hde', k_float * tail_decay.T[:, :, None], v_float, precision=exact_precision)

def linear_layer(q_float, k_float, v_float, log_decay):
    length = BLK_DEV * BLOCK
    shards = SEQUENCE_LENGTH // length

    def split_rows(values):
        return values.reshape(shards, length, HEADS, HEAD_DIM)
    decays = log_decay.reshape(HEADS, shards, length).transpose(1, 0, 2)

    def advance(state_now, pieces):
        query_rows, key_rows, value_rows, decay_rows = pieces
        cumulative = jnp.cumsum(decay_rows, axis=1)
        output_rows = shard_output(query_rows, key_rows, value_rows, cumulative, state_now)
        state_next = jnp.exp(cumulative[:, -1])[:, None, None] * state_now + shard_state(key_rows, value_rows, cumulative)
        return (state_next, output_rows)
    start_state = jnp.zeros((HEADS, HEAD_DIM, HEAD_DIM), q_float.dtype)
    final_state, outputs = lax.scan(advance, start_state, (split_rows(q_float), split_rows(k_float), split_rows(v_float), decays))
    raw_out = outputs.reshape(SEQUENCE_LENGTH, HEADS, HEAD_DIM)
    mean_square = lax.optimization_barrier(jnp.mean(raw_out * raw_out, axis=(1, 2), keepdims=True))
    return raw_out / jnp.sqrt(mean_square + norm_epsilon)

def rounded(values):
    return lax.optimization_barrier(values.astype(jnp.bfloat16)).astype(jnp.float32)

def softmax_layer(query_two, key_two, values_two, out_grad, doc_ids):
    length = BLK_DEV * BLOCK
    shards = SEQUENCE_LENGTH // length
    window = (REACH + 1) * length
    margin = REACH * length
    scale = 1.0 / math.sqrt(HEAD_DIM)
    token_doc = jnp.repeat(doc_ids.astype(jnp.int32), BLOCK)
    q_float = query_two.astype(jnp.float32)
    grad_float = out_grad.astype(jnp.float32)
    padding = jnp.zeros((margin, HEADS, HEAD_DIM), jnp.float32)
    k_padded = jnp.concatenate([padding, key_two.astype(jnp.float32)], axis=0)
    v_padded = jnp.concatenate([padding, values_two.astype(jnp.float32)], axis=0)
    doc_padded = jnp.concatenate([jnp.full((margin,), -1, jnp.int32), token_doc])
    pos_padded = jnp.arange(SEQUENCE_LENGTH + margin, dtype=jnp.int32) - margin

    def visit(totals, shard):
        key_total, value_total = totals
        start = (shard * length).astype(jnp.int32)
        query_rows = lax.dynamic_slice_in_dim(q_float, start, length, 0)
        grad_rows = lax.dynamic_slice_in_dim(grad_float, start, length, 0)
        query_doc = lax.dynamic_slice_in_dim(token_doc, start, length, 0)
        query_pos = start + jnp.arange(length, dtype=jnp.int32)
        key_rows = lax.dynamic_slice_in_dim(k_padded, start, window, 0)
        value_rows = lax.dynamic_slice_in_dim(v_padded, start, window, 0)
        key_doc = lax.dynamic_slice_in_dim(doc_padded, start, window, 0)
        key_pos = lax.dynamic_slice_in_dim(pos_padded, start, window, 0)
        allowed = (key_pos[None, :] <= query_pos[:, None]) & (key_pos[None, :] >= 0) & (key_doc[None, :] == query_doc[:, None])
        scores = jnp.einsum('thd,uhd->htu', query_rows, key_rows) * scale
        scores = jnp.where(allowed[None], scores, floor_score)
        peak = lax.optimization_barrier(jnp.max(scores, axis=2, keepdims=True))
        mass = lax.optimization_barrier(jnp.sum(jnp.where(allowed[None], jnp.exp(scores - peak), 0.0), axis=2, keepdims=True))
        log_mass = peak + jnp.log(mass)
        prob = jnp.where(allowed[None], jnp.exp(scores - log_mass), 0.0)
        prob_low = rounded(prob)
        attended = jnp.einsum('htu,uhd->thd', prob_low, value_rows)
        delta = lax.optimization_barrier(jnp.sum(grad_rows * attended, axis=2))
        grad_prob = jnp.einsum('thd,uhd->htu', grad_rows, value_rows)
        grad_score = rounded(prob * (grad_prob - delta.T[:, :, None]) * scale)
        query_grad = jnp.einsum('htu,uhd->thd', grad_score, key_rows)
        key_grad = jnp.einsum('htu,thd->uhd', grad_score, query_rows)
        value_grad = jnp.einsum('htu,thd->uhd', prob_low, grad_rows)
        key_total = lax.dynamic_update_slice_in_dim(key_total, lax.dynamic_slice_in_dim(key_total, start, window, 0) + key_grad, start, 0)
        value_total = lax.dynamic_update_slice_in_dim(value_total, lax.dynamic_slice_in_dim(value_total, start, window, 0) + value_grad, start, 0)
        return ((key_total, value_total), query_grad)
    zero_total = jnp.zeros((SEQUENCE_LENGTH + margin, HEADS, HEAD_DIM), jnp.float32)
    totals, query_grads = lax.scan(visit, (zero_total, zero_total), jnp.arange(shards, dtype=jnp.int32))
    grad_query_two = query_grads.reshape(SEQUENCE_LENGTH, HEADS, HEAD_DIM)
    return (grad_query_two, totals[0][margin:], totals[1][margin:])

def reference(query_one, key_one, value_one, log_decay, query_two, key_two, out_grad, doc_ids):

    def forward_one(q_float, k_float, v_float):
        return linear_layer(q_float, k_float, v_float, log_decay)
    normed, pull_back = jax.vjp(forward_one, query_one.astype(jnp.float32), key_one.astype(jnp.float32), value_one.astype(jnp.float32))
    values_two = normed.astype(jnp.bfloat16)
    grad_query_two, grad_key_two, grad_values_two = softmax_layer(query_two, key_two, values_two, out_grad, doc_ids)
    grad_query_one, grad_key_one, grad_value_one = pull_back(grad_values_two)
    return (grad_query_one, grad_key_one, grad_value_one, grad_query_two, grad_key_two)
```

```python
from functools import partial
import math

import jax
import jax.numpy as jnp
from jax import lax
from jax.experimental import pallas as pl
from jax.experimental.pallas import tpu as pltpu
from jax.sharding import PartitionSpec as P

BLOCK = 128
REACH = 8


exact_precision = lax.Precision.HIGHEST
floor_score = -1e30
norm_epsilon = 1e-05


def prefix(value, axis, join, neutral, backward):
    count, mine = (lax.axis_size(axis), lax.axis_index(axis))
    pieces = jax.tree.map(lambda part: lax.all_gather(part, axis), value)
    if backward:
        pieces = jax.tree.map(lambda part: part[::-1], pieces)
        mine = count - 1 - mine
    total = jax.tree.map(
        lambda part, zero: jnp.full_like(part, 0) + jnp.asarray(zero, part.dtype), value, neutral
    )

    def hop(position, total):
        longer = join(total, jax.tree.map(lambda part: part[position], pieces))
        return jax.tree.map(lambda new, old: jnp.where(position < mine, new, old), longer, total)

    return lax.fori_loop(0, count - 1, hop, total)


def from_behind(block, axis, distance):
    devices = range(lax.axis_size(axis))
    route = [(i - distance, i) for i in devices if i - distance in devices]
    return lax.ppermute(block, axis, route)


def for_sending(shard):
    return jax.tree.map(lambda a: a.astype(jnp.bfloat16) if a.dtype == jnp.float32 else a, shard)


def lower_mask(length):
    return lax.broadcasted_iota(jnp.int32, (length, length), 0) >= lax.broadcasted_iota(
        jnp.int32, (length, length), 1
    )


def shard_output(q_float, k_float, v_float, cumulative, incoming):
    lower = lower_mask(q_float.shape[0])[None]
    gaps = cumulative[:, :, None] - cumulative[:, None, :]
    weights = jnp.where(lower, jnp.exp(jnp.where(lower, gaps, 0.0)), 0.0)
    scores = jnp.einsum("thd,uhd->htu", q_float, k_float, precision=exact_precision) * weights
    inner_part = jnp.einsum("htu,uhe->the", scores, v_float, precision=exact_precision)
    outer_part = jnp.einsum(
        "thd,hde->the",
        q_float * jnp.exp(cumulative).T[:, :, None],
        incoming,
        precision=exact_precision,
    )
    return inner_part + outer_part


def shard_state(k_float, v_float, cumulative):
    tail_decay = jnp.exp(cumulative[:, -1:] - cumulative)
    return jnp.einsum(
        "uhd,uhe->hde", k_float * tail_decay.T[:, :, None], v_float, precision=exact_precision
    )


def chain_join(earlier, later):
    return (earlier[0] * later[0], later[0][:, None, None] * earlier[1] + later[1])


def scores_work(query_two, keys_block, allowed, scale):
    raw_scores = (
        jnp.einsum("thd,uhd->htu", query_two, keys_block, preferred_element_type=jnp.float32)
        * scale
    )
    return jnp.where(allowed[None], raw_scores, floor_score)


def probs_work(tile_scores, log_mass, allowed, values_block):
    prob = jnp.where(allowed[None], jnp.exp(tile_scores - log_mass[:, :, None]), 0.0)
    part_out = jnp.einsum(
        "htu,uhd->thd", prob.astype(jnp.bfloat16), values_block, preferred_element_type=jnp.float32
    )
    return (prob, part_out)


def grads_work(prob, query_two, out_grad, keys_block, values_block, delta, scale):
    grad_prob = jnp.einsum(
        "thd,uhd->htu", out_grad, values_block, preferred_element_type=jnp.float32
    )
    grad_score = (prob * (grad_prob - delta.T[:, :, None]) * scale).astype(jnp.bfloat16)
    query_grad = jnp.einsum(
        "htu,uhd->thd", grad_score, keys_block, preferred_element_type=jnp.float32
    )
    key_grad = jnp.einsum("htu,thd->uhd", grad_score, query_two, preferred_element_type=jnp.float32)
    value_grad = jnp.einsum(
        "htu,thd->uhd", prob.astype(jnp.bfloat16), out_grad, preferred_element_type=jnp.float32
    )
    return (query_grad, key_grad, value_grad)


def ring_body(query_one, key_one, value_one, log_decay, query_two, key_two, out_grad, doc_ids):
    length, heads_here, width = query_one.shape
    shards = lax.axis_size("seq")
    token_position = lax.axis_index("seq")
    features = heads_here * lax.axis_size("head") * width
    q_float = query_one.astype(jnp.float32)
    k_float = key_one.astype(jnp.float32)
    v_float = value_one.astype(jnp.float32)
    cumulative = jnp.cumsum(log_decay, axis=1)
    carry_decay = jnp.exp(cumulative[:, -1])
    local_state, state_pull = jax.vjp(partial(shard_state, cumulative=cumulative), k_float, v_float)
    identity = (jnp.ones_like(carry_decay), jnp.zeros_like(local_state))
    incoming = prefix((carry_decay, local_state), "seq", chain_join, identity, False)[1]
    raw_out, output_pull = jax.vjp(
        partial(shard_output, cumulative=cumulative, incoming=incoming), q_float, k_float, v_float
    )
    square_sum = lax.psum(jnp.sum(raw_out * raw_out, axis=(1, 2)), "head")
    inverse = 1.0 / jnp.sqrt(square_sum / features + norm_epsilon)
    normed = raw_out * inverse[:, None, None]
    values_two = normed.astype(jnp.bfloat16)
    blocks_here = length // BLOCK
    scale = 1.0 / math.sqrt(width)
    offsets = jnp.arange(length, dtype=jnp.int32)
    query_doc = jnp.repeat(
        lax.dynamic_slice_in_dim(doc_ids, token_position * blocks_here, blocks_here), BLOCK
    )
    query_pos = token_position * length + offsets
    masks = []
    for distance in range(REACH + 1):
        source = (token_position - distance) % shards
        key_doc = jnp.repeat(
            lax.dynamic_slice_in_dim(doc_ids, source * blocks_here, blocks_here), BLOCK
        )
        key_pos = source * length + offsets
        masks.append(
            (key_pos[None, :] <= query_pos[:, None]) & (key_doc[None, :] == query_doc[:, None])
        )
    blocks = [(key_two, values_two)]
    current = (key_two, values_two)
    for distance in range(1, REACH + 1):
        current = from_behind((current[0], current[1]), "seq", 1)
        blocks.append(current)
    row_shape = (length, heads_here, width)
    peak_now = jnp.full((heads_here, length), floor_score, jnp.float32)
    mass_now = jnp.zeros((heads_here, length), jnp.float32)
    tile_list = []
    for distance in range(REACH + 1):
        allowed = masks[distance]
        tile_scores = scores_work(query_two, blocks[distance][0], allowed, scale)
        peak_next = jnp.maximum(peak_now, jnp.max(tile_scores, axis=2))
        fresh_mass = jnp.sum(
            jnp.where(allowed[None], jnp.exp(tile_scores - peak_next[:, :, None]), 0.0), axis=2
        )
        mass_now = mass_now * jnp.exp(peak_now - peak_next) + fresh_mass
        peak_now = peak_next
        tile_list.append(tile_scores)
    log_mass = peak_now + jnp.log(mass_now)
    attended = jnp.zeros(row_shape, jnp.float32)
    prob_list = []
    for distance in range(REACH + 1):
        allowed = masks[distance]
        prob, part_out = probs_work(tile_list[distance], log_mass, allowed, blocks[distance][1])
        attended = attended + part_out
        prob_list.append(prob)
    delta = jnp.sum(out_grad.astype(jnp.float32) * attended, axis=2)
    grad_query_two = jnp.zeros(row_shape, jnp.float32)
    carried = None
    for distance in range(REACH, -1, -1):
        keys_block, values_block = blocks[distance]
        query_grad, key_grad, value_grad = grads_work(
            prob_list[distance], query_two, out_grad, keys_block, values_block, delta, scale
        )
        grad_query_two = grad_query_two + query_grad
        if carried is None:
            carried = (key_grad, value_grad)
        else:
            moved = jax.tree.map(
                lambda part, own: part.astype(own.dtype),
                from_behind(for_sending(carried), "seq", -1),
                carried,
            )
            carried = (moved[0] + key_grad, moved[1] + value_grad)
    grad_key_two, grad_values_two = carried
    cross_sum = lax.psum(jnp.sum(raw_out * grad_values_two, axis=(1, 2)), "head")
    grad_raw = (
        inverse[:, None, None] * grad_values_two
        - raw_out * (inverse**3 * cross_sum / features)[:, None, None]
    )
    direct_state = jnp.einsum(
        "thd,the->hde",
        q_float * jnp.exp(cumulative).T[:, :, None],
        grad_raw,
        precision=exact_precision,
    )
    later_grad = prefix((carry_decay, direct_state), "seq", chain_join, identity, True)[1]
    grad_query_one, grad_key_out, grad_value_out = output_pull(grad_raw)
    grad_key_state, grad_value_state = state_pull(later_grad)
    return (
        grad_query_one,
        grad_key_out + grad_key_state,
        grad_value_out + grad_value_state,
        grad_query_two,
        grad_key_two,
    )


f32, bf16 = (jnp.float32, jnp.bfloat16)
LOG2E = math.log2(math.e)
PART_ROWS = 16


def dot(a, b):
    return lax.dot_general(a, b, (((1,), (0,)), ((), ())), preferred_element_type=f32)


def dot_nt(a, b):
    return lax.dot_general(a, b, (((1,), (1,)), ((), ())), preferred_element_type=f32)


def dot_tn(a, b):
    return lax.dot_general(a, b, (((0,), (0,)), ((), ())), preferred_element_type=f32)


def two_parts(value):
    high = value.astype(bf16)
    return high, (value - high.astype(f32)).astype(bf16)


def row_sums(value):
    ones = jnp.ones((PART_ROWS, value.shape[1]), bf16)
    high, low = two_parts(value)
    return dot_nt(ones, high) + dot_nt(ones, low)


def chunk_decays(parts):
    lower = lower_mask(BLOCK)
    log_row = jnp.sum(parts.astype(f32), axis=0, keepdims=True)
    column = jnp.sum(jnp.where(lower, log_row, 0.0), axis=1, keepdims=True)
    upper = lax.broadcasted_iota(jnp.int32, (BLOCK, BLOCK), 0) <= lax.broadcasted_iota(
        jnp.int32, (BLOCK, BLOCK), 1
    )
    row = jnp.sum(dot(parts, jnp.where(upper, 1.0, 0.0).astype(bf16)), axis=0, keepdims=True)
    last = column[BLOCK - 1 : BLOCK, :]
    weights = jnp.exp(jnp.where(lower, column - row, floor_score))
    return weights, jnp.exp(column), jnp.exp(last - column), jnp.exp(last)


def linear_forward(first_ref, raw_ref, state_ref, sums_ref):
    chunks = first_ref.shape[0]
    width = first_ref.shape[2]
    rows = lax.broadcasted_iota(jnp.int32, (chunks, BLOCK), 0)
    state = jnp.zeros((width, width), f32)
    sums = jnp.zeros((chunks, BLOCK), f32)
    for c in range(chunks):
        q = first_ref[c, 0:BLOCK, :]
        k = first_ref[c, BLOCK : 2 * BLOCK, :]
        v = first_ref[c, 2 * BLOCK : 3 * BLOCK, :]
        weights, grow, tail, whole = chunk_decays(first_ref[c, 3 * BLOCK :, :])
        prob = (dot_nt(q, k) * weights).astype(bf16)
        state_low = state.astype(bf16)
        raw = dot(prob, v) + grow * dot(q, state_low)
        state_ref[c] = state_low
        state = whole * state + dot_tn(k, (v.astype(f32) * tail).astype(bf16))
        raw_ref[c * BLOCK : (c + 1) * BLOCK, :] = raw
        sums = sums + jnp.where(rows == c, row_sums(raw * raw)[0:1, :], 0.0)
    high, low = two_parts(sums)
    sums_ref[0:chunks, :] = high
    sums_ref[chunks : 2 * chunks, :] = low


def softmax_both(
    features, starts_ref, second_ref, raw_ref, sums_ref, out_ref, value_grad_ref,
    key_s, key_t_s, value_s, value_t_s, key_grad_s,
):
    chunks = second_ref.shape[0]
    width = second_ref.shape[2]
    scale = 1.0 / math.sqrt(width)
    inverse = 1.0 / jnp.sqrt(sums_ref[...] / features + norm_epsilon)
    columns = inverse.T
    for c in range(chunks):
        here = slice(c * BLOCK, (c + 1) * BLOCK)
        k = second_ref[c, BLOCK : 2 * BLOCK, :]
        v = (raw_ref[here, :] * columns[:, c : c + 1]).astype(bf16)
        key_s[here, :] = k
        key_t_s[:, here] = k.T
        value_s[here, :] = v
        value_t_s[:, here] = v.T
    key_grad_s[...] = jnp.zeros_like(key_grad_s)
    value_grad_ref[...] = jnp.zeros_like(value_grad_ref)

    def window(t, first, blocks):
        length = blocks * BLOCK
        begin = pl.multiple_of(jnp.maximum(t - (blocks - 1), 0) * BLOCK, BLOCK)
        rows = pl.ds(begin, length)
        q = second_ref[t, 0:BLOCK, :]
        g = second_ref[t, 2 * BLOCK : 3 * BLOCK, :]
        q_t, g_t = (q.T, g.T)
        scores = dot(key_s[rows, :], q_t) * (scale * LOG2E)
        u_pos = begin + lax.broadcasted_iota(jnp.int32, (length, BLOCK), 0)
        t_pos = t * BLOCK + lax.broadcasted_iota(jnp.int32, (length, BLOCK), 1)
        allowed = (u_pos <= t_pos) & (u_pos >= first * BLOCK)
        scores = jnp.where(allowed, scores, floor_score)
        peak = jnp.max(scores, axis=0, keepdims=True)
        mass = jnp.exp2(scores - peak)
        prob = mass * (1.0 / jnp.sum(mass, axis=0, keepdims=True))
        prob_low = prob.astype(bf16)
        attended = dot(value_t_s[:, rows], prob_low)
        delta = jnp.sum(g_t.astype(f32) * attended, axis=0, keepdims=True)
        grad_prob = dot(value_s[rows, :], g_t)
        grad_score = (prob * (grad_prob - delta) * scale).astype(bf16)
        out_ref[t, 0:BLOCK, :] = dot(key_t_s[:, rows], grad_score).T.astype(bf16)
        key_grad_s[rows, :] += dot(grad_score, q)
        value_grad_ref[rows, :] += dot(prob_low, g)

    def step(t, carry):
        first = starts_ref[t]
        need = t - first + 1
        sizes = [n for n in (1, 2, 4, 8) if n <= chunks]
        least = 0
        for n in sizes:
            pl.when((need > least) & (need <= n))(partial(window, t, first, n))
            least = n
        return carry

    lax.fori_loop(0, chunks, step, 0)
    rows = lax.broadcasted_iota(jnp.int32, (chunks, BLOCK), 0)
    cross = jnp.zeros((chunks, BLOCK), f32)
    for c in range(chunks):
        here = slice(c * BLOCK, (c + 1) * BLOCK)
        out_ref[c, BLOCK : 2 * BLOCK, :] = key_grad_s[here, :].astype(bf16)
        part = row_sums(raw_ref[here, :] * value_grad_ref[here, :])[0:1, :]
        cross = cross + jnp.where(rows == c, part, 0.0)
    high, low = two_parts(cross)
    for c in range(chunks):
        out_ref[c, 2 * BLOCK : 2 * BLOCK + chunks, :] = high
        out_ref[c, 2 * BLOCK + chunks :, :] = low


def linear_backward(
    features, first_ref, raw_ref, state_ref, sums_ref, cross_ref, value_grad_ref, out_ref
):
    chunks = first_ref.shape[0]
    width = first_ref.shape[2]
    inverse = 1.0 / jnp.sqrt(sums_ref[...] / features + norm_epsilon)
    inverse_columns = inverse.T
    cross_columns = (inverse * inverse * inverse * cross_ref[...] / features).T
    state_grad = jnp.zeros((width, width), f32)
    for c in range(chunks - 1, -1, -1):
        here = slice(c * BLOCK, (c + 1) * BLOCK)
        q = first_ref[c, 0:BLOCK, :]
        k = first_ref[c, BLOCK : 2 * BLOCK, :]
        v = first_ref[c, 2 * BLOCK : 3 * BLOCK, :]
        weights, grow, tail, whole = chunk_decays(first_ref[c, 3 * BLOCK :, :])
        grad = (
            inverse_columns[:, c : c + 1] * value_grad_ref[here, :]
            - raw_ref[here, :] * cross_columns[:, c : c + 1]
        )
        grad_low = grad.astype(bf16)
        grad_grown = (grad * grow).astype(bf16)
        prob = (dot_nt(q, k) * weights).astype(bf16)
        grad_score = (dot_nt(grad_low, v) * weights).astype(bf16)
        state_low = state_grad.astype(bf16)
        query_grad = dot(grad_score, k) + grow * dot_nt(grad_low, state_ref[c])
        key_grad = dot_tn(grad_score, q) + tail * dot_nt(v, state_low)
        value_grad = dot_tn(prob, grad_low) + tail * dot(k, state_low)
        state_grad = whole * state_grad + dot_tn(q, grad_grown)
        out_ref[c, 0:BLOCK, :] = query_grad.astype(bf16)
        out_ref[c, BLOCK : 2 * BLOCK, :] = key_grad.astype(bf16)
        out_ref[c, 2 * BLOCK : 3 * BLOCK, :] = value_grad.astype(bf16)


def call(kernel, outs, scratch, *operands, prefetch=0):
    vmem = pl.BlockSpec(memory_space=pltpu.VMEM)
    smem = pl.BlockSpec(memory_space=pltpu.SMEM)
    return pl.pallas_call(
        kernel,
        out_shape=[jax.ShapeDtypeStruct(shape, kind) for shape, kind in outs],
        in_specs=[smem] * prefetch + [vmem] * (len(operands) - prefetch),
        out_specs=[vmem] * len(outs),
        scratch_shapes=[pltpu.VMEM(shape, kind) for shape, kind in scratch],
        compiler_params=pltpu.CompilerParams(vmem_limit_bytes=40 * 1024 * 1024),
    )(*operands)


def heads_first(x):
    return jnp.swapaxes(x, 0, 1)


def exchange(x):
    return lax.all_to_all(x, "seq", 0, 0, tiled=True)


def three_parts(x):
    high = lax.reduce_precision(x, 8, 7)
    middle = lax.reduce_precision(x - high, 8, 7)
    return [part.astype(bf16) for part in (high, middle, x - high - middle)]


def over_heads(received, chunks):
    parts = received.astype(f32)
    mine = jnp.sum(parts[:, 0:chunks] + parts[:, chunks : 2 * chunks], axis=0)
    count = lax.axis_size("head")
    total = mine
    for step in range(1, count):
        total = total + lax.ppermute(mine, "head", [(i, (i + step) % count) for i in range(count)])
    return total


def body(query_one, key_one, value_one, log_decay, query_two, key_two, out_grad, doc_ids):
    length, heads_here, width = query_one.shape
    shards = lax.axis_size("seq")
    if heads_here != shards or length != BLOCK or shards % 16 or width != BLOCK:
        return ring_body(
            query_one, key_one, value_one, log_decay, query_two, key_two, out_grad, doc_ids
        )
    positions = shards * length
    features = heads_here * lax.axis_size("head") * width
    decay_rows = jnp.stack(three_parts(log_decay), axis=1)
    decay_rows = jnp.pad(decay_rows, ((0, 0), (0, PART_ROWS - 3), (0, 0)))
    first = exchange(
        jnp.concatenate([heads_first(x) for x in (query_one, key_one, value_one)] + [decay_rows], axis=1)
    )
    raw, states, sums = call(
        linear_forward,
        [((positions, width), f32), ((shards, width, width), bf16), ((2 * shards, BLOCK), bf16)],
        [],
        first,
    )
    sums_rows = jnp.broadcast_to(sums[None], (shards,) + sums.shape)
    second = exchange(
        jnp.concatenate([heads_first(x) for x in (query_two, key_two, out_grad)] + [sums_rows], axis=1)
    )
    square_sums = over_heads(second[:, 3 * BLOCK :], shards)
    starts = jnp.sum((doc_ids[None, :] < doc_ids[:, None]).astype(jnp.int32), axis=1)
    third, value_grad = call(
        partial(softmax_both, features),
        [((shards, 2 * BLOCK + 2 * shards, width), bf16), ((positions, width), f32)],
        [
            ((positions, width), bf16),
            ((width, positions), bf16),
            ((positions, width), bf16),
            ((width, positions), bf16),
            ((positions, width), f32),
        ],
        starts,
        second,
        raw,
        square_sums,
        prefetch=1,
    )
    third = exchange(third)
    cross = over_heads(third[:, 2 * BLOCK :], shards)
    (fourth,) = call(
        partial(linear_backward, features),
        [((shards, 3 * BLOCK, width), bf16)],
        [],
        first,
        raw,
        states,
        square_sums,
        cross,
        value_grad,
    )
    fourth = exchange(fourth)

    def result(received, place):
        return heads_first(received[:, place * BLOCK : (place + 1) * BLOCK]).astype(f32)

    return (
        result(fourth, 0),
        result(fourth, 1),
        result(fourth, 2),
        result(third, 0),
        result(third, 1),
    )


def solution(mesh):
    placed = (
        P("seq", "head", None),
        P("seq", "head", None),
        P("seq", "head", None),
        P("head", "seq"),
        P("seq", "head", None),
        P("seq", "head", None),
        P("seq", "head", None),
        P(),
    )
    return jax.shard_map(
        body,
        mesh=mesh,
        in_specs=placed,
        out_specs=(P("seq", "head", None),) * 5,
        check_vma=False,
    )
```

```python
from functools import partial
import math

import jax
import jax.numpy as jnp
from jax import lax
from jax.experimental import pallas as pl
from jax.experimental.pallas import tpu as pltpu
from jax.sharding import PartitionSpec as P

BLOCK = 128
REACH = 8


exact_precision = lax.Precision.HIGHEST
floor_score = -1e30
norm_epsilon = 1e-05


def prefix(value, axis, join, neutral, backward):
    count, mine = (lax.axis_size(axis), lax.axis_index(axis))
    pieces = jax.tree.map(lambda part: lax.all_gather(part, axis), value)
    if backward:
        pieces = jax.tree.map(lambda part: part[::-1], pieces)
        mine = count - 1 - mine
    total = jax.tree.map(
        lambda part, zero: jnp.full_like(part, 0) + jnp.asarray(zero, part.dtype), value, neutral
    )

    def hop(position, total):
        longer = join(total, jax.tree.map(lambda part: part[position], pieces))
        return jax.tree.map(lambda new, old: jnp.where(position < mine, new, old), longer, total)

    return lax.fori_loop(0, count - 1, hop, total)


def from_behind(block, axis, distance):
    devices = range(lax.axis_size(axis))
    route = [(i - distance, i) for i in devices if i - distance in devices]
    return lax.ppermute(block, axis, route)


def for_sending(shard):
    return jax.tree.map(lambda a: a.astype(jnp.bfloat16) if a.dtype == jnp.float32 else a, shard)


def lower_mask(length):
    return lax.broadcasted_iota(jnp.int32, (length, length), 0) >= lax.broadcasted_iota(
        jnp.int32, (length, length), 1
    )


def shard_output(q_float, k_float, v_float, cumulative, incoming):
    lower = lower_mask(q_float.shape[0])[None]
    gaps = cumulative[:, :, None] - cumulative[:, None, :]
    weights = jnp.where(lower, jnp.exp(jnp.where(lower, gaps, 0.0)), 0.0)
    scores = jnp.einsum("thd,uhd->htu", q_float, k_float, precision=exact_precision) * weights
    inner_part = jnp.einsum("htu,uhe->the", scores, v_float, precision=exact_precision)
    outer_part = jnp.einsum(
        "thd,hde->the",
        q_float * jnp.exp(cumulative).T[:, :, None],
        incoming,
        precision=exact_precision,
    )
    return inner_part + outer_part


def shard_state(k_float, v_float, cumulative):
    tail_decay = jnp.exp(cumulative[:, -1:] - cumulative)
    return jnp.einsum(
        "uhd,uhe->hde", k_float * tail_decay.T[:, :, None], v_float, precision=exact_precision
    )


def chain_join(earlier, later):
    return (earlier[0] * later[0], later[0][:, None, None] * earlier[1] + later[1])


def scores_work(query_two, keys_block, allowed, scale):
    raw_scores = (
        jnp.einsum("thd,uhd->htu", query_two, keys_block, preferred_element_type=jnp.float32)
        * scale
    )
    return jnp.where(allowed[None], raw_scores, floor_score)


def probs_work(tile_scores, log_mass, allowed, values_block):
    prob = jnp.where(allowed[None], jnp.exp(tile_scores - log_mass[:, :, None]), 0.0)
    part_out = jnp.einsum(
        "htu,uhd->thd", prob.astype(jnp.bfloat16), values_block, preferred_element_type=jnp.float32
    )
    return (prob, part_out)


def grads_work(prob, query_two, out_grad, keys_block, values_block, delta, scale):
    grad_prob = jnp.einsum(
        "thd,uhd->htu", out_grad, values_block, preferred_element_type=jnp.float32
    )
    grad_score = (prob * (grad_prob - delta.T[:, :, None]) * scale).astype(jnp.bfloat16)
    query_grad = jnp.einsum(
        "htu,uhd->thd", grad_score, keys_block, preferred_element_type=jnp.float32
    )
    key_grad = jnp.einsum("htu,thd->uhd", grad_score, query_two, preferred_element_type=jnp.float32)
    value_grad = jnp.einsum(
        "htu,thd->uhd", prob.astype(jnp.bfloat16), out_grad, preferred_element_type=jnp.float32
    )
    return (query_grad, key_grad, value_grad)


def ring_body(query_one, key_one, value_one, log_decay, query_two, key_two, out_grad, doc_ids):
    length, heads_here, width = query_one.shape
    shards = lax.axis_size("seq")
    token_position = lax.axis_index("seq")
    features = heads_here * lax.axis_size("head") * width
    q_float = query_one.astype(jnp.float32)
    k_float = key_one.astype(jnp.float32)
    v_float = value_one.astype(jnp.float32)
    cumulative = jnp.cumsum(log_decay, axis=1)
    carry_decay = jnp.exp(cumulative[:, -1])
    local_state, state_pull = jax.vjp(partial(shard_state, cumulative=cumulative), k_float, v_float)
    identity = (jnp.ones_like(carry_decay), jnp.zeros_like(local_state))
    incoming = prefix((carry_decay, local_state), "seq", chain_join, identity, False)[1]
    raw_out, output_pull = jax.vjp(
        partial(shard_output, cumulative=cumulative, incoming=incoming), q_float, k_float, v_float
    )
    square_sum = lax.psum(jnp.sum(raw_out * raw_out, axis=(1, 2)), "head")
    inverse = 1.0 / jnp.sqrt(square_sum / features + norm_epsilon)
    normed = raw_out * inverse[:, None, None]
    values_two = normed.astype(jnp.bfloat16)
    blocks_here = length // BLOCK
    scale = 1.0 / math.sqrt(width)
    offsets = jnp.arange(length, dtype=jnp.int32)
    query_doc = jnp.repeat(
        lax.dynamic_slice_in_dim(doc_ids, token_position * blocks_here, blocks_here), BLOCK
    )
    query_pos = token_position * length + offsets
    masks = []
    for distance in range(REACH + 1):
        source = (token_position - distance) % shards
        key_doc = jnp.repeat(
            lax.dynamic_slice_in_dim(doc_ids, source * blocks_here, blocks_here), BLOCK
        )
        key_pos = source * length + offsets
        masks.append(
            (key_pos[None, :] <= query_pos[:, None]) & (key_doc[None, :] == query_doc[:, None])
        )
    blocks = [(key_two, values_two)]
    current = (key_two, values_two)
    for distance in range(1, REACH + 1):
        current = from_behind((current[0], current[1]), "seq", 1)
        blocks.append(current)
    row_shape = (length, heads_here, width)
    peak_now = jnp.full((heads_here, length), floor_score, jnp.float32)
    mass_now = jnp.zeros((heads_here, length), jnp.float32)
    tile_list = []
    for distance in range(REACH + 1):
        allowed = masks[distance]
        tile_scores = scores_work(query_two, blocks[distance][0], allowed, scale)
        peak_next = jnp.maximum(peak_now, jnp.max(tile_scores, axis=2))
        fresh_mass = jnp.sum(
            jnp.where(allowed[None], jnp.exp(tile_scores - peak_next[:, :, None]), 0.0), axis=2
        )
        mass_now = mass_now * jnp.exp(peak_now - peak_next) + fresh_mass
        peak_now = peak_next
        tile_list.append(tile_scores)
    log_mass = peak_now + jnp.log(mass_now)
    attended = jnp.zeros(row_shape, jnp.float32)
    prob_list = []
    for distance in range(REACH + 1):
        allowed = masks[distance]
        prob, part_out = probs_work(tile_list[distance], log_mass, allowed, blocks[distance][1])
        attended = attended + part_out
        prob_list.append(prob)
    delta = jnp.sum(out_grad.astype(jnp.float32) * attended, axis=2)
    grad_query_two = jnp.zeros(row_shape, jnp.float32)
    carried = None
    for distance in range(REACH, -1, -1):
        keys_block, values_block = blocks[distance]
        query_grad, key_grad, value_grad = grads_work(
            prob_list[distance], query_two, out_grad, keys_block, values_block, delta, scale
        )
        grad_query_two = grad_query_two + query_grad
        if carried is None:
            carried = (key_grad, value_grad)
        else:
            moved = jax.tree.map(
                lambda part, own: part.astype(own.dtype),
                from_behind(for_sending(carried), "seq", -1),
                carried,
            )
            carried = (moved[0] + key_grad, moved[1] + value_grad)
    grad_key_two, grad_values_two = carried
    cross_sum = lax.psum(jnp.sum(raw_out * grad_values_two, axis=(1, 2)), "head")
    grad_raw = (
        inverse[:, None, None] * grad_values_two
        - raw_out * (inverse**3 * cross_sum / features)[:, None, None]
    )
    direct_state = jnp.einsum(
        "thd,the->hde",
        q_float * jnp.exp(cumulative).T[:, :, None],
        grad_raw,
        precision=exact_precision,
    )
    later_grad = prefix((carry_decay, direct_state), "seq", chain_join, identity, True)[1]
    grad_query_one, grad_key_out, grad_value_out = output_pull(grad_raw)
    grad_key_state, grad_value_state = state_pull(later_grad)
    return (
        grad_query_one,
        grad_key_out + grad_key_state,
        grad_value_out + grad_value_state,
        grad_query_two,
        grad_key_two,
    )


f32, bf16 = (jnp.float32, jnp.bfloat16)
LOG2E = math.log2(math.e)
PART_ROWS = 16


def dot(a, b):
    return lax.dot_general(a, b, (((1,), (0,)), ((), ())), preferred_element_type=f32)


def dot_nt(a, b):
    return lax.dot_general(a, b, (((1,), (1,)), ((), ())), preferred_element_type=f32)


def dot_tn(a, b):
    return lax.dot_general(a, b, (((0,), (0,)), ((), ())), preferred_element_type=f32)


def two_parts(value):
    high = value.astype(bf16)
    return high, (value - high.astype(f32)).astype(bf16)


def row_sums(value):
    ones = jnp.ones((PART_ROWS, value.shape[1]), bf16)
    high, low = two_parts(value)
    return dot_nt(ones, high) + dot_nt(ones, low)


def chunk_decays(parts):
    lower = lower_mask(BLOCK)
    log_row = jnp.sum(parts.astype(f32), axis=0, keepdims=True)
    column = jnp.sum(jnp.where(lower, log_row, 0.0), axis=1, keepdims=True)
    upper = lax.broadcasted_iota(jnp.int32, (BLOCK, BLOCK), 0) <= lax.broadcasted_iota(
        jnp.int32, (BLOCK, BLOCK), 1
    )
    row = jnp.sum(dot(parts, jnp.where(upper, 1.0, 0.0).astype(bf16)), axis=0, keepdims=True)
    last = column[BLOCK - 1 : BLOCK, :]
    weights = jnp.exp(jnp.where(lower, column - row, floor_score))
    return weights, jnp.exp(column), jnp.exp(last - column), jnp.exp(last)


def lightning_piece(ref, place):
    arrays = [ref[place, n * BLOCK : (n + 1) * BLOCK, :] for n in range(3)]
    return arrays + [chunk_decays(ref[place, ref.shape[1] - PART_ROWS :, :])]


UNROLL = 16


def over_chunks(chunks, body, carry, backward=False):
    unrolled = math.gcd(UNROLL, chunks)

    def step(n, carry):
        for part in range(unrolled):
            c = n * unrolled + part
            carry = body(chunks - 1 - c if backward else c, carry)
        return carry

    if unrolled == chunks:
        return step(0, carry)
    return lax.fori_loop(0, chunks // unrolled, step, carry)


def block_rows(c):
    if isinstance(c, int):
        return slice(c * BLOCK, (c + 1) * BLOCK)
    return pl.ds(pl.multiple_of(c * BLOCK, BLOCK), BLOCK)


def linear_state(heads, second_ref, state_ref):
    chunks, width = (second_ref.shape[0] // heads, second_ref.shape[2])

    def chunk(c, states):
        following = []
        for head in range(heads):
            _, k, v, (_, _, tail, whole) = lightning_piece(second_ref, c * heads + head)
            following.append(
                whole * states[head] + dot_tn(k, (v.astype(f32) * tail).astype(bf16))
            )
        return tuple(following)

    states = over_chunks(chunks, chunk, (jnp.zeros((width, width), f32),) * heads)
    for head in range(heads):
        state_ref[head] = states[head]


def value_gradient(half, kept_ref, other_ref, head, c):
    return jnp.where(
        half == head, kept_ref[block_rows(c), :], other_ref[block_rows(c), :].astype(f32)
    )


def linear_forward(
    heads, info_ref, second_ref, incoming_ref, kept_ref, other_ref,
    raw_ref, sent_ref, state_ref, sums_ref,
):
    chunks = second_ref.shape[0] // heads
    half = info_ref[info_ref.shape[0] - 1]

    def chunk(c, states):
        following = []
        squares, cross = (0.0, 0.0)
        raws = []
        for head in range(heads):
            q, k, v, (weights, grow, tail, whole) = lightning_piece(second_ref, c * heads + head)
            prob = (dot_nt(q, k) * weights).astype(bf16)
            state_low = states[head].astype(bf16)
            raw = dot(prob, v) + grow * dot(q, state_low)
            state_ref[head, c] = state_low
            following.append(
                whole * states[head] + dot_tn(k, (v.astype(f32) * tail).astype(bf16))
            )
            raw_ref[head, block_rows(c), :] = raw
            raws.append(raw)
            grad = value_gradient(half, kept_ref, other_ref, head, c)
            squares = squares + row_sums(raw * raw)[0:1, :]
            cross = cross + row_sums(raw * grad)[0:1, :]
        sent_ref[block_rows(c), :] = jnp.where(half == 0, raws[1], raws[0]).astype(bf16)
        sums_ref[c : c + 1, :] = squares
        sums_ref[chunks + c : chunks + c + 1, :] = cross
        return tuple(following)

    over_chunks(chunks, chunk, tuple(incoming_ref[head] for head in range(heads)))


def column(columns, c):
    if isinstance(c, int):
        return columns[:, c : c + 1]
    lanes = lax.broadcasted_iota(jnp.int32, columns.shape, 1)
    return jnp.sum(jnp.where(lanes == c, columns, 0.0), axis=1, keepdims=True)


def norm_columns(features, sums_ref):
    chunks = sums_ref.shape[0] // 2
    inverse = 1.0 / jnp.sqrt(sums_ref[0:chunks, :] / features + norm_epsilon)
    return inverse.T, (inverse * inverse * inverse * sums_ref[chunks:, :] / features).T


def linear_state_grad(
    features, heads, info_ref, second_ref, raw_ref, sums_ref, kept_ref, other_ref, state_grad_ref
):
    chunks, width = (second_ref.shape[0] // heads, second_ref.shape[2])
    half = info_ref[info_ref.shape[0] - 1]
    inverse, cross = norm_columns(features, sums_ref)

    def chunk(c, grads):
        following = []
        for head in range(heads):
            q, _, _, (_, grow, _, whole) = lightning_piece(second_ref, c * heads + head)
            grad = column(inverse, c) * value_gradient(half, kept_ref, other_ref, head, c)
            grad = grad - raw_ref[head, block_rows(c), :] * column(cross, c)
            following.append(whole * grads[head] + dot_tn(q, (grad * grow).astype(bf16)))
        return tuple(following)

    grads = over_chunks(chunks, chunk, (jnp.zeros((width, width), f32),) * heads, True)
    for head in range(heads):
        state_grad_ref[head] = grads[head]


def linear_backward(
    features, heads, info_ref, second_ref, raw_ref, state_ref, sums_ref, kept_ref, other_ref, later_ref,
    out_ref,
):
    chunks = second_ref.shape[0] // heads
    half = info_ref[info_ref.shape[0] - 1]
    inverse, cross = norm_columns(features, sums_ref)

    def chunk(c, grads):
        following = []
        for head in range(heads):
            place = c * heads + head
            q, k, v, (weights, grow, tail, whole) = lightning_piece(second_ref, place)
            grad = column(inverse, c) * value_gradient(half, kept_ref, other_ref, head, c)
            grad = grad - raw_ref[head, block_rows(c), :] * column(cross, c)
            grad_low = grad.astype(bf16)
            prob = (dot_nt(q, k) * weights).astype(bf16)
            grad_score = (dot_nt(grad_low, v) * weights).astype(bf16)
            state_low = grads[head].astype(bf16)
            query_grad = dot(grad_score, k) + grow * dot_nt(grad_low, state_ref[head, c])
            key_grad = dot_tn(grad_score, q) + tail * dot_nt(v, state_low)
            value_grad = dot_tn(prob, grad_low) + tail * dot(k, state_low)
            following.append(whole * grads[head] + dot_tn(q, (grad * grow).astype(bf16)))
            out_ref[place, 0:BLOCK, :] = query_grad.astype(bf16)
            out_ref[place, BLOCK : 2 * BLOCK, :] = key_grad.astype(bf16)
            out_ref[place, 2 * BLOCK : 3 * BLOCK, :] = value_grad.astype(bf16)
        return tuple(following)

    over_chunks(chunks, chunk, tuple(later_ref[head] for head in range(heads)), True)


TOGETHER = 4
GROUP = TOGETHER * BLOCK


def by_window(info_ref, chunks, window):
    def step(group, carry):
        end = TOGETHER * (group + 1)
        need = end - info_ref[TOGETHER * group]
        least = 0
        for blocks in window_sizes(chunks):
            begin = pl.multiple_of((end - blocks) * BLOCK, 2 * BLOCK)
            pl.when((need > least) & (need <= blocks))(partial(window, group, begin, blocks))
            least = blocks
        return carry

    lax.fori_loop(0, chunks // TOGETHER, step, 0)


def window_sizes(chunks):
    return range(TOGETHER, min(chunks, REACH + TOGETHER) + 1, 2)


def window_scores(info_ref, keys, queries, group, begin):
    shape = (keys.shape[0], queries.shape[0])
    scores = dot(keys, queries.T) * (LOG2E / math.sqrt(keys.shape[1]))
    u_pos = begin + lax.broadcasted_iota(jnp.int32, shape, 0)
    lane = lax.broadcasted_iota(jnp.int32, (1, shape[1]), 1)
    lowest = jnp.zeros_like(lane)
    for n in range(TOGETHER):
        lowest = jnp.where(lane >= n * BLOCK, info_ref[TOGETHER * group + n] * BLOCK, lowest)
    return scores, (u_pos >= lowest) & (u_pos <= group * GROUP + lane)


def group_rows(group):
    return pl.ds(pl.multiple_of(group * GROUP, GROUP), GROUP)


def softmax_masses(info_ref, first_ref, mass_ref, kept_ref, sent_ref, key_s, query_s, grad_s, value_grad_s):
    chunks, width = (first_ref.shape[0], first_ref.shape[2])
    for c in range(chunks):
        here = block_rows(c)
        query_s[here, :] = first_ref[c, 0:BLOCK, :]
        key_s[here, :] = first_ref[c, BLOCK : 2 * BLOCK, :]
        grad_s[here, :] = first_ref[c, 2 * BLOCK :, :]
        value_grad_s[here, :] = jnp.zeros((BLOCK, width), f32)

    def window(group, begin, blocks):
        rows = pl.ds(begin, blocks * BLOCK)
        scores, allowed = window_scores(
            info_ref, key_s[rows, :], query_s[group_rows(group), :], group, begin
        )
        scores = jnp.where(allowed, scores, floor_score)
        peak = jnp.max(scores, axis=0, keepdims=True)
        mass = jnp.exp2(scores - peak)
        total = jnp.sum(mass, axis=0, keepdims=True)
        mass_ref[pl.ds(group, 1), :] = peak + jnp.log2(total)
        prob = (mass * (1.0 / total)).astype(bf16)
        value_grad_s[rows, :] += dot(prob, grad_s[group_rows(group), :])

    by_window(info_ref, chunks, window)
    half = info_ref[info_ref.shape[0] - 1]
    for c in range(chunks // 2):
        low = value_grad_s[block_rows(c), :]
        high = value_grad_s[block_rows(chunks // 2 + c), :]
        kept_ref[block_rows(c), :] = jnp.where(half == 0, low, high)
        sent_ref[block_rows(c), :] = jnp.where(half == 0, high, low).astype(bf16)


def softmax_grads(
    features, info_ref, first_ref, mass_ref, raw_ref, other_ref, sums_ref, other_sums_ref, out_ref,
    key_s, key_t_s, value_s, value_t_s, query_s, grad_s, key_grad_s,
):
    chunks, width = (first_ref.shape[0], first_ref.shape[2])
    side = chunks // 2
    scale = 1.0 / math.sqrt(width)
    half = info_ref[info_ref.shape[0] - 1]
    inverse, other_inverse = [
        (1.0 / jnp.sqrt(ref[0:side, :] / features + norm_epsilon)).T for ref in (sums_ref, other_sums_ref)
    ]
    for c in range(chunks):
        here = block_rows(c)
        there = block_rows(c % side)
        own = jnp.where(half == 0, raw_ref[0, there, :], raw_ref[1, there, :])
        own = own * column(inverse, c % side)
        other = other_ref[there, :].astype(f32) * column(other_inverse, c % side)
        v = jnp.where(half == c // side, own, other).astype(bf16)
        value_s[here, :] = v
        value_t_s[:, here] = v.T
        query_s[here, :] = first_ref[c, 0:BLOCK, :]
        key_s[here, :] = first_ref[c, BLOCK : 2 * BLOCK, :]
        key_t_s[:, here] = first_ref[c, BLOCK : 2 * BLOCK, :].T
        grad_s[here, :] = first_ref[c, 2 * BLOCK :, :]
        key_grad_s[here, :] = jnp.zeros((BLOCK, width), f32)

    def window(group, begin, blocks):
        rows = pl.ds(begin, blocks * BLOCK)
        queries = query_s[group_rows(group), :]
        scores, allowed = window_scores(info_ref, key_s[rows, :], queries, group, begin)
        scores = jnp.where(allowed, scores - mass_ref[pl.ds(group, 1), :], floor_score)
        prob = jnp.exp2(scores)
        g_t = grad_s[group_rows(group), :].T
        attended = dot(value_t_s[:, rows], prob.astype(bf16))
        delta = jnp.sum(g_t.astype(f32) * attended, axis=0, keepdims=True)
        grad_prob = dot(value_s[rows, :], g_t)
        grad_score = (prob * ((grad_prob - delta) * scale)).astype(bf16)
        key_grad_s[rows, :] += dot(grad_score, queries)
        query_grad = dot(key_t_s[:, rows], grad_score).T.astype(bf16)
        for c in range(TOGETHER):
            out_ref[TOGETHER * group + c, 0:BLOCK, :] = query_grad[block_rows(c), :]

    by_window(info_ref, chunks, window)
    for c in range(chunks):
        out_ref[c, BLOCK : 2 * BLOCK, :] = key_grad_s[block_rows(c), :].astype(bf16)


def call(kernel, micros, outs, scratch, *operands, prefetch=0, room=8, whole=False):
    vmem = pl.BlockSpec(memory_space=pltpu.VMEM)
    smem = pl.BlockSpec(memory_space=pltpu.SMEM)
    results = [jax.ShapeDtypeStruct(shape, kind) for shape, kind in outs]
    held = [jax.ShapeDtypeStruct(shape, kind) for shape, kind in scratch]
    size = sum(
        a.size * a.dtype.itemsize for a in [*held, *(([*operands, *results]) if whole else [])]
    )
    return pl.pallas_call(
        kernel,
        out_shape=results,
        in_specs=[smem] * prefetch + [vmem] * (len(operands) - prefetch),
        out_specs=[vmem] * len(outs),
        scratch_shapes=[pltpu.VMEM(shape, kind) for shape, kind in scratch],
        compiler_params=pltpu.CompilerParams(vmem_limit_bytes=size + room * 1024 * 1024),
        cost_estimate=pl.CostEstimate(
            flops=int(micros * 1e9), bytes_accessed=int(micros * 3e6), transcendentals=0
        ),
    )(*operands)


def swap_matrix(chunks):
    size = chunks * chunks
    i = lax.broadcasted_iota(jnp.int32, (size, size), 0)
    j = lax.broadcasted_iota(jnp.int32, (size, size), 1)
    return jnp.where(j == (i % chunks) * chunks + i // chunks, 1.0, 0.0).astype(bf16)


def pair_order(heads):
    return [(h % 2) * (heads // 2) + h // 2 for h in range(heads)]


def pack(order, *refs):
    arrays, out_ref = ([ref for ref in refs[:-1] if len(ref.shape) == 3], refs[-1])
    length, heads, width = arrays[0].shape
    swap = swap_matrix(heads)
    for place, ref in enumerate(arrays):
        for begin in range(0, length, heads):
            rows = ref[begin : begin + heads].reshape(heads * heads, width)
            swapped = dot(swap, rows).astype(bf16)
            row = place * length + begin
            for h in range(heads):
                out_ref[order[h], row : row + heads, :] = swapped[h * heads : (h + 1) * heads, :]
    if len(arrays) == len(refs) - 1:
        return
    decay_ref = refs[-2]
    high, _ = two_parts(decay_ref[...])
    middle, last = two_parts(decay_ref[...] - high.astype(f32))
    row = lax.broadcasted_iota(jnp.int32, (PART_ROWS, length), 0)
    for h in range(heads):
        tile = jnp.zeros((PART_ROWS, length), f32)
        for n, part in enumerate((high, middle, last)):
            tile = jnp.where(row == n, part[h : h + 1, :].astype(f32), tile)
        out_ref[order[h], len(arrays) * length :, :] = tile.astype(bf16)


def unpack(order, in_ref, *outs):
    length, heads, width = outs[0].shape
    swap = swap_matrix(heads)
    for place, out_ref in enumerate(outs):
        for begin in range(0, length, heads):
            row = place * length + begin
            rows = jnp.concatenate(
                [in_ref[order[h], row : row + heads, :] for h in range(heads)], axis=0
            )
            out_ref[begin : begin + heads] = dot(swap, rows).reshape(heads, heads, width)


def exchange(x):
    return lax.all_to_all(x, "seq", 0, 0, tiled=True)


def exchange_half(x):
    side = lax.axis_size("seq") // 2
    groups = [list(range(side)), list(range(side, 2 * side))]
    return lax.all_to_all(x, "seq", 0, 0, tiled=True, axis_index_groups=groups)


def upward(x):
    side = lax.axis_size("seq") // 2
    return lax.ppermute(x, "seq", [(i, i + side) for i in range(side)])


def downward(x):
    side = lax.axis_size("seq") // 2
    return lax.ppermute(x, "seq", [(i + side, i) for i in range(side)])


def swapped(x):
    side = lax.axis_size("seq") // 2
    return lax.ppermute(x, "seq", [(i, (i + side) % (2 * side)) for i in range(2 * side)])


def over_heads(mine):
    count = lax.axis_size("head")
    total = mine
    for step in range(1, count):
        total = total + lax.ppermute(mine, "head", [(i, (i + step) % count) for i in range(count)])
    return total


def body(query_one, key_one, value_one, log_decay, query_two, key_two, out_grad, doc_ids):
    length, heads_here, width = query_one.shape
    shards = lax.axis_size("seq")
    if heads_here != shards or length != BLOCK or shards != 16 or width != BLOCK:
        return ring_body(
            query_one, key_one, value_one, log_decay, query_two, key_two, out_grad, doc_ids
        )
    side = shards // 2
    heads = heads_here // side
    half_length = side * length
    features = heads_here * lax.axis_size("head") * width
    half = (lax.axis_index("seq") >= side).astype(jnp.int32)
    starts = jnp.sum((doc_ids[None, :] < doc_ids[:, None]).astype(jnp.int32), axis=1)
    info = jnp.concatenate([starts, half[None]])
    straight, paired = (list(range(heads_here)), pair_order(heads_here))

    def packed(order, rows, arrays, *more):
        arrays = [pltpu.with_memory_space_constraint(array, pltpu.HBM) for array in arrays]
        return call(
            partial(pack, order), 3, [((heads_here, rows, width), bf16)], [], *arrays, *more, whole=True
        )[0]

    first = exchange(packed(paired, 3 * length, (query_two, key_two, out_grad)))
    second = exchange_half(
        packed(straight, 3 * length + PART_ROWS, (query_one, key_one, value_one), log_decay)
    )
    half_rows = (half_length, width)
    full_rows = (shards * length, width)
    masses, grad_kept, grad_sent = call(
        softmax_masses,
        6,
        [
            ((shards // TOGETHER, GROUP), f32),
            (half_rows, f32),
            (half_rows, bf16),
        ],
        [(full_rows, bf16), (full_rows, bf16), (full_rows, bf16), (full_rows, f32)],
        info,
        first,
        prefetch=1,
    )
    grad_other = swapped(grad_sent)
    state_shape = (heads, width, width)
    (state,) = call(partial(linear_state, heads), 1, [(state_shape, f32)], [], second)
    incoming = upward(state)
    raw, raw_sent, states, sums = call(
        partial(linear_forward, heads),
        4,
        [
            ((heads, half_length, width), f32),
            (half_rows, bf16),
            ((heads, side, width, width), bf16),
            ((2 * side, BLOCK), f32),
        ],
        [],
        info,
        second,
        incoming,
        grad_kept,
        grad_other,
        prefetch=1,
    )
    raw_other = swapped(raw_sent)
    sums = exchange_half(jnp.broadcast_to(sums[None], (side,) + sums.shape))
    sums = over_heads(jnp.sum(sums, axis=0))
    sums_other = swapped(sums[:side])
    (softmax_grad,) = call(
        partial(softmax_grads, features),
        7,
        [((shards, 2 * BLOCK, width), bf16)],
        [
            (full_rows, bf16),
            ((width, shards * length), bf16),
            (full_rows, bf16),
            ((width, shards * length), bf16),
            (full_rows, bf16),
            (full_rows, bf16),
            (full_rows, f32),
        ],
        info,
        first,
        masses,
        raw,
        raw_other,
        sums,
        sums_other,
        prefetch=1,
    )
    (state_grad,) = call(
        partial(linear_state_grad, features, heads),
        2,
        [(state_shape, f32)],
        [],
        info,
        second,
        raw,
        sums,
        grad_kept,
        grad_other,
        prefetch=1,
    )
    later_grad = downward(state_grad)
    later_grad, softmax_grad = lax.optimization_barrier((later_grad, softmax_grad))
    softmax_grad = exchange(softmax_grad)
    (linear_grads,) = call(
        partial(linear_backward, features, heads),
        5,
        [((heads_here, 3 * BLOCK, width), bf16)],
        [],
        info,
        second,
        raw,
        states,
        sums,
        grad_kept,
        grad_other,
        later_grad,
        prefetch=1,
    )
    softmax_grad, linear_grads = lax.optimization_barrier((softmax_grad, linear_grads))
    linear_grads = exchange_half(linear_grads)

    def unpacked(order, count, received):
        outs = [((length, heads_here, width), f32)] * count
        return call(partial(unpack, order), count, outs, [], received, whole=True)

    query_one_grad, key_one_grad, value_one_grad = unpacked(straight, 3, linear_grads)
    query_two_grad, key_two_grad = unpacked(paired, 2, softmax_grad)
    return (query_one_grad, key_one_grad, value_one_grad, query_two_grad, key_two_grad)


def solution(mesh):
    placed = (
        P("seq", "head", None),
        P("seq", "head", None),
        P("seq", "head", None),
        P("head", "seq"),
        P("seq", "head", None),
        P("seq", "head", None),
        P("seq", "head", None),
        P(),
    )
    return jax.shard_map(
        body,
        mesh=mesh,
        in_specs=placed,
        out_specs=(P("seq", "head", None),) * 5,
        check_vma=False,
    )
```

```python
from functools import partial
import math

import jax
import jax.numpy as jnp
from jax import lax
from jax.experimental import pallas as pl
from jax.experimental.pallas import tpu as pltpu
from jax.sharding import PartitionSpec as P

BLOCK = 128
REACH = 8


exact_precision = lax.Precision.HIGHEST
floor_score = -1e30
norm_epsilon = 1e-05


def prefix(value, axis, join, neutral, backward):
    count, mine = (lax.axis_size(axis), lax.axis_index(axis))
    pieces = jax.tree.map(lambda part: lax.all_gather(part, axis), value)
    if backward:
        pieces = jax.tree.map(lambda part: part[::-1], pieces)
        mine = count - 1 - mine
    total = jax.tree.map(
        lambda part, zero: jnp.full_like(part, 0) + jnp.asarray(zero, part.dtype), value, neutral
    )

    def hop(position, total):
        longer = join(total, jax.tree.map(lambda part: part[position], pieces))
        return jax.tree.map(lambda new, old: jnp.where(position < mine, new, old), longer, total)

    return lax.fori_loop(0, count - 1, hop, total)


def from_behind(block, axis, distance):
    devices = range(lax.axis_size(axis))
    route = [(i - distance, i) for i in devices if i - distance in devices]
    return lax.ppermute(block, axis, route)


def for_sending(shard):
    return jax.tree.map(lambda a: a.astype(jnp.bfloat16) if a.dtype == jnp.float32 else a, shard)


def lower_mask(length):
    return lax.broadcasted_iota(jnp.int32, (length, length), 0) >= lax.broadcasted_iota(
        jnp.int32, (length, length), 1
    )


def shard_output(q_float, k_float, v_float, cumulative, incoming):
    lower = lower_mask(q_float.shape[0])[None]
    gaps = cumulative[:, :, None] - cumulative[:, None, :]
    weights = jnp.where(lower, jnp.exp(jnp.where(lower, gaps, 0.0)), 0.0)
    scores = jnp.einsum("thd,uhd->htu", q_float, k_float, precision=exact_precision) * weights
    inner_part = jnp.einsum("htu,uhe->the", scores, v_float, precision=exact_precision)
    outer_part = jnp.einsum(
        "thd,hde->the",
        q_float * jnp.exp(cumulative).T[:, :, None],
        incoming,
        precision=exact_precision,
    )
    return inner_part + outer_part


def shard_state(k_float, v_float, cumulative):
    tail_decay = jnp.exp(cumulative[:, -1:] - cumulative)
    return jnp.einsum(
        "uhd,uhe->hde", k_float * tail_decay.T[:, :, None], v_float, precision=exact_precision
    )


def chain_join(earlier, later):
    return (earlier[0] * later[0], later[0][:, None, None] * earlier[1] + later[1])


def scores_work(query_two, keys_block, allowed, scale):
    raw_scores = (
        jnp.einsum("thd,uhd->htu", query_two, keys_block, preferred_element_type=jnp.float32)
        * scale
    )
    return jnp.where(allowed[None], raw_scores, floor_score)


def probs_work(tile_scores, log_mass, allowed, values_block):
    prob = jnp.where(allowed[None], jnp.exp(tile_scores - log_mass[:, :, None]), 0.0)
    part_out = jnp.einsum(
        "htu,uhd->thd", prob.astype(jnp.bfloat16), values_block, preferred_element_type=jnp.float32
    )
    return (prob, part_out)


def grads_work(prob, query_two, out_grad, keys_block, values_block, delta, scale):
    grad_prob = jnp.einsum(
        "thd,uhd->htu", out_grad, values_block, preferred_element_type=jnp.float32
    )
    grad_score = (prob * (grad_prob - delta.T[:, :, None]) * scale).astype(jnp.bfloat16)
    query_grad = jnp.einsum(
        "htu,uhd->thd", grad_score, keys_block, preferred_element_type=jnp.float32
    )
    key_grad = jnp.einsum("htu,thd->uhd", grad_score, query_two, preferred_element_type=jnp.float32)
    value_grad = jnp.einsum(
        "htu,thd->uhd", prob.astype(jnp.bfloat16), out_grad, preferred_element_type=jnp.float32
    )
    return (query_grad, key_grad, value_grad)


def ring_body(query_one, key_one, value_one, log_decay, query_two, key_two, out_grad, doc_ids):
    length, heads_here, width = query_one.shape
    shards = lax.axis_size("seq")
    token_position = lax.axis_index("seq")
    features = heads_here * lax.axis_size("head") * width
    q_float = query_one.astype(jnp.float32)
    k_float = key_one.astype(jnp.float32)
    v_float = value_one.astype(jnp.float32)
    cumulative = jnp.cumsum(log_decay, axis=1)
    carry_decay = jnp.exp(cumulative[:, -1])
    local_state, state_pull = jax.vjp(partial(shard_state, cumulative=cumulative), k_float, v_float)
    identity = (jnp.ones_like(carry_decay), jnp.zeros_like(local_state))
    incoming = prefix((carry_decay, local_state), "seq", chain_join, identity, False)[1]
    raw_out, output_pull = jax.vjp(
        partial(shard_output, cumulative=cumulative, incoming=incoming), q_float, k_float, v_float
    )
    square_sum = lax.psum(jnp.sum(raw_out * raw_out, axis=(1, 2)), "head")
    inverse = 1.0 / jnp.sqrt(square_sum / features + norm_epsilon)
    normed = raw_out * inverse[:, None, None]
    values_two = normed.astype(jnp.bfloat16)
    blocks_here = length // BLOCK
    scale = 1.0 / math.sqrt(width)
    offsets = jnp.arange(length, dtype=jnp.int32)
    query_doc = jnp.repeat(
        lax.dynamic_slice_in_dim(doc_ids, token_position * blocks_here, blocks_here), BLOCK
    )
    query_pos = token_position * length + offsets
    masks = []
    for distance in range(REACH + 1):
        source = (token_position - distance) % shards
        key_doc = jnp.repeat(
            lax.dynamic_slice_in_dim(doc_ids, source * blocks_here, blocks_here), BLOCK
        )
        key_pos = source * length + offsets
        masks.append(
            (key_pos[None, :] <= query_pos[:, None]) & (key_doc[None, :] == query_doc[:, None])
        )
    blocks = [(key_two, values_two)]
    current = (key_two, values_two)
    for distance in range(1, REACH + 1):
        current = from_behind((current[0], current[1]), "seq", 1)
        blocks.append(current)
    row_shape = (length, heads_here, width)
    peak_now = jnp.full((heads_here, length), floor_score, jnp.float32)
    mass_now = jnp.zeros((heads_here, length), jnp.float32)
    tile_list = []
    for distance in range(REACH + 1):
        allowed = masks[distance]
        tile_scores = scores_work(query_two, blocks[distance][0], allowed, scale)
        peak_next = jnp.maximum(peak_now, jnp.max(tile_scores, axis=2))
        fresh_mass = jnp.sum(
            jnp.where(allowed[None], jnp.exp(tile_scores - peak_next[:, :, None]), 0.0), axis=2
        )
        mass_now = mass_now * jnp.exp(peak_now - peak_next) + fresh_mass
        peak_now = peak_next
        tile_list.append(tile_scores)
    log_mass = peak_now + jnp.log(mass_now)
    attended = jnp.zeros(row_shape, jnp.float32)
    prob_list = []
    for distance in range(REACH + 1):
        allowed = masks[distance]
        prob, part_out = probs_work(tile_list[distance], log_mass, allowed, blocks[distance][1])
        attended = attended + part_out
        prob_list.append(prob)
    delta = jnp.sum(out_grad.astype(jnp.float32) * attended, axis=2)
    grad_query_two = jnp.zeros(row_shape, jnp.float32)
    carried = None
    for distance in range(REACH, -1, -1):
        keys_block, values_block = blocks[distance]
        query_grad, key_grad, value_grad = grads_work(
            prob_list[distance], query_two, out_grad, keys_block, values_block, delta, scale
        )
        grad_query_two = grad_query_two + query_grad
        if carried is None:
            carried = (key_grad, value_grad)
        else:
            moved = jax.tree.map(
                lambda part, own: part.astype(own.dtype),
                from_behind(for_sending(carried), "seq", -1),
                carried,
            )
            carried = (moved[0] + key_grad, moved[1] + value_grad)
    grad_key_two, grad_values_two = carried
    cross_sum = lax.psum(jnp.sum(raw_out * grad_values_two, axis=(1, 2)), "head")
    grad_raw = (
        inverse[:, None, None] * grad_values_two
        - raw_out * (inverse**3 * cross_sum / features)[:, None, None]
    )
    direct_state = jnp.einsum(
        "thd,the->hde",
        q_float * jnp.exp(cumulative).T[:, :, None],
        grad_raw,
        precision=exact_precision,
    )
    later_grad = prefix((carry_decay, direct_state), "seq", chain_join, identity, True)[1]
    grad_query_one, grad_key_out, grad_value_out = output_pull(grad_raw)
    grad_key_state, grad_value_state = state_pull(later_grad)
    return (
        grad_query_one,
        grad_key_out + grad_key_state,
        grad_value_out + grad_value_state,
        grad_query_two,
        grad_key_two,
    )


f32, bf16 = (jnp.float32, jnp.bfloat16)
LOG2E = math.log2(math.e)
PART_ROWS = 16


def dot(a, b):
    return lax.dot_general(a, b, (((1,), (0,)), ((), ())), preferred_element_type=f32)


def dot_nt(a, b):
    return lax.dot_general(a, b, (((1,), (1,)), ((), ())), preferred_element_type=f32)


def dot_tn(a, b):
    return lax.dot_general(a, b, (((0,), (0,)), ((), ())), preferred_element_type=f32)


def two_parts(value):
    high = value.astype(bf16)
    return high, (value - high.astype(f32)).astype(bf16)


def row_sums(value):
    ones = jnp.ones((PART_ROWS, value.shape[1]), bf16)
    high, low = two_parts(value)
    return dot_nt(ones, high) + dot_nt(ones, low)


def decay_column(parts):
    log_row = jnp.sum(parts.astype(f32), axis=0, keepdims=True)
    return jnp.sum(jnp.where(lower_mask(BLOCK), log_row, 0.0), axis=1, keepdims=True)


def chunk_decays(parts):
    lower = lower_mask(BLOCK)
    column = decay_column(parts)
    upper = lax.broadcasted_iota(jnp.int32, (BLOCK, BLOCK), 0) <= lax.broadcasted_iota(
        jnp.int32, (BLOCK, BLOCK), 1
    )
    row = jnp.sum(dot(parts, jnp.where(upper, 1.0, 0.0).astype(bf16)), axis=0, keepdims=True)
    last = column[BLOCK - 1 : BLOCK, :]
    weights = jnp.exp(jnp.where(lower, column - row, floor_score))
    return weights, jnp.exp(column), jnp.exp(last - column), jnp.exp(last)


def lightning_piece(ref, place):
    arrays = [ref[place, n * BLOCK : (n + 1) * BLOCK, :] for n in range(3)]
    return arrays + [chunk_decays(ref[place, ref.shape[1] - PART_ROWS :, :])]


UNROLL = 16


def over_chunks(chunks, body, carry, backward=False):
    unrolled = math.gcd(UNROLL, chunks)

    def step(n, carry):
        for part in range(unrolled):
            c = n * unrolled + part
            carry = body(chunks - 1 - c if backward else c, carry)
        return carry

    if unrolled == chunks:
        return step(0, carry)
    return lax.fori_loop(0, chunks // unrolled, step, carry)


def block_rows(c):
    if isinstance(c, int):
        return slice(c * BLOCK, (c + 1) * BLOCK)
    return pl.ds(pl.multiple_of(c * BLOCK, BLOCK), BLOCK)


def linear_state(heads, second_ref, state_ref):
    chunks, width = (second_ref.shape[0] // heads, second_ref.shape[2])

    def chunk(c, states):
        following = []
        for head in range(heads):
            _, k, v, (_, _, tail, whole) = lightning_piece(second_ref, c * heads + head)
            following.append(
                whole * states[head] + dot_tn(k, (v.astype(f32) * tail).astype(bf16))
            )
        return tuple(following)

    states = over_chunks(chunks, chunk, (jnp.zeros((width, width), f32),) * heads)
    for head in range(heads):
        state_ref[head] = states[head]


def value_gradient(half, kept_ref, other_ref, head, c):
    return jnp.where(
        half == head, kept_ref[block_rows(c), :], other_ref[block_rows(c), :].astype(f32)
    )


def linear_local(heads, second_ref, raw_ref):
    chunks, width = (second_ref.shape[0] // heads, second_ref.shape[2])

    def chunk(c, states):
        following = []
        for head in range(heads):
            q, k, v, (weights, grow, tail, whole) = lightning_piece(second_ref, c * heads + head)
            prob = (dot_nt(q, k) * weights).astype(bf16)
            raw = dot(prob, v) + grow * dot(q, states[head].astype(bf16))
            raw_ref[head, block_rows(c), :] = raw
            following.append(
                whole * states[head] + dot_tn(k, (v.astype(f32) * tail).astype(bf16))
            )
        return tuple(following)

    over_chunks(chunks, chunk, (jnp.zeros((width, width), f32),) * heads)


def linear_output(
    heads, info_ref, second_ref, incoming_ref, local_ref, kept_ref, other_ref, raw_ref, sent_ref, sums_ref
):
    chunks = second_ref.shape[0] // heads
    half = info_ref[info_ref.shape[0] - 1]
    incoming = [incoming_ref[head].astype(bf16) for head in range(heads)]
    carried = [jnp.ones((1, 1), f32)] * heads
    for c in range(chunks):
        here = block_rows(c)
        raws = []
        squares, products = (0.0, 0.0)
        for head in range(heads):
            place = c * heads + head
            logs = decay_column(second_ref[place, second_ref.shape[1] - PART_ROWS :, :])
            outer = dot(second_ref[place, 0:BLOCK, :], incoming[head])
            raw = local_ref[head, here, :] + (carried[head] * jnp.exp(logs)) * outer
            carried[head] = carried[head] * jnp.exp(logs[BLOCK - 1 : BLOCK, :])
            grad = value_gradient(half, kept_ref, other_ref, head, c)
            squares = squares + raw * raw
            products = products + raw * grad
            raws.append(raw.astype(bf16))
            raw_ref[head, here, :] = raws[head]
        sent_ref[here, :] = jnp.where(half == 0, raws[1], raws[0])
        sums_ref[c : c + 1, :] = row_sums(squares)[0:1, :]
        sums_ref[chunks + c : chunks + c + 1, :] = row_sums(products)[0:1, :]


def column(columns, c):
    if isinstance(c, int):
        return columns[:, c : c + 1]
    lanes = lax.broadcasted_iota(jnp.int32, columns.shape, 1)
    return jnp.sum(jnp.where(lanes == c, columns, 0.0), axis=1, keepdims=True)


def norm_columns(features, sums_ref):
    chunks = sums_ref.shape[0] // 2
    inverse = 1.0 / jnp.sqrt(sums_ref[0:chunks, :] / features + norm_epsilon)
    return inverse.T, (inverse * inverse * inverse * sums_ref[chunks:, :] / features).T


def linear_state_grad(
    features, heads, info_ref, second_ref, raw_ref, sums_ref, kept_ref, other_ref, state_grad_ref
):
    chunks, width = (second_ref.shape[0] // heads, second_ref.shape[2])
    half = info_ref[info_ref.shape[0] - 1]
    inverse, cross = norm_columns(features, sums_ref)

    def chunk(c, grads):
        following = []
        for head in range(heads):
            q, _, _, (_, grow, _, whole) = lightning_piece(second_ref, c * heads + head)
            grad = column(inverse, c) * value_gradient(half, kept_ref, other_ref, head, c)
            grad = grad - raw_ref[head, block_rows(c), :].astype(f32) * column(cross, c)
            following.append(whole * grads[head] + dot_tn(q, (grad * grow).astype(bf16)))
        return tuple(following)

    grads = over_chunks(chunks, chunk, (jnp.zeros((width, width), f32),) * heads, True)
    for head in range(heads):
        state_grad_ref[head] = grads[head]


def linear_backward(
    features, heads, info_ref, second_ref, raw_ref, incoming_ref, sums_ref, kept_ref, other_ref, later_ref,
    out_ref, state_s,
):
    chunks = second_ref.shape[0] // heads

    def before(c, states):
        following = []
        for head in range(heads):
            _, k, v, (_, _, tail, whole) = lightning_piece(second_ref, c * heads + head)
            state_s[head, c] = states[head].astype(bf16)
            following.append(
                whole * states[head] + dot_tn(k, (v.astype(f32) * tail).astype(bf16))
            )
        return tuple(following)

    over_chunks(chunks, before, tuple(incoming_ref[head] for head in range(heads)))
    half = info_ref[info_ref.shape[0] - 1]
    inverse, cross = norm_columns(features, sums_ref)

    def chunk(c, grads):
        following = []
        for head in range(heads):
            place = c * heads + head
            q, k, v, (weights, grow, tail, whole) = lightning_piece(second_ref, place)
            grad = column(inverse, c) * value_gradient(half, kept_ref, other_ref, head, c)
            grad = grad - raw_ref[head, block_rows(c), :].astype(f32) * column(cross, c)
            grad_low = grad.astype(bf16)
            prob = (dot_nt(q, k) * weights).astype(bf16)
            grad_score = (dot_nt(grad_low, v) * weights).astype(bf16)
            state_low = grads[head].astype(bf16)
            query_grad = dot(grad_score, k) + grow * dot_nt(grad_low, state_s[head, c])
            key_grad = dot_tn(grad_score, q) + tail * dot_nt(v, state_low)
            value_grad = dot_tn(prob, grad_low) + tail * dot(k, state_low)
            following.append(whole * grads[head] + dot_tn(q, (grad * grow).astype(bf16)))
            out_ref[place, 0:BLOCK, :] = query_grad.astype(bf16)
            out_ref[place, BLOCK : 2 * BLOCK, :] = key_grad.astype(bf16)
            out_ref[place, 2 * BLOCK : 3 * BLOCK, :] = value_grad.astype(bf16)
        return tuple(following)

    over_chunks(chunks, chunk, tuple(later_ref[head] for head in range(heads)), True)


TOGETHER = 4
GROUP = TOGETHER * BLOCK


def by_window(info_ref, chunks, window):
    def step(group, carry):
        end = TOGETHER * (group + 1)
        need = end - info_ref[TOGETHER * group]
        least = 0
        for blocks in window_sizes(chunks):
            begin = end - blocks
            pl.when((need > least) & (need <= blocks))(partial(window, group, begin, blocks))
            least = blocks
        return carry

    lax.fori_loop(0, chunks // TOGETHER, step, 0)


def window_sizes(chunks):
    return range(TOGETHER, min(chunks, REACH + TOGETHER) + 1, 2)


def window_scores(info_ref, keys, queries, group, begin):
    shape = (keys.shape[0], queries.shape[0])
    scores = dot(keys, queries.T) * (LOG2E / math.sqrt(keys.shape[1]))
    u_pos = begin + lax.broadcasted_iota(jnp.int32, shape, 0)
    lane = lax.broadcasted_iota(jnp.int32, (1, shape[1]), 1)
    lowest = jnp.zeros_like(lane)
    for n in range(TOGETHER):
        lowest = jnp.where(lane >= n * BLOCK, info_ref[TOGETHER * group + n] * BLOCK, lowest)
    return scores, (u_pos >= lowest) & (u_pos <= group * GROUP + lane)


def blocks_of(first_ref, place, block, count):
    rows = first_ref[pl.ds(block, count), place * BLOCK : (place + 1) * BLOCK, :]
    return rows.reshape(count * BLOCK, first_ref.shape[2])


def softmax_masses(info_ref, first_ref, mass_ref, kept_ref, sent_ref, value_grad_s):
    chunks, width = (first_ref.shape[0], first_ref.shape[2])
    value_grad_s[...] = jnp.zeros_like(value_grad_s)

    def window(group, begin, blocks):
        rows = pl.ds(pl.multiple_of(begin * BLOCK, 2 * BLOCK), blocks * BLOCK)
        scores, allowed = window_scores(
            info_ref,
            blocks_of(first_ref, 1, begin, blocks),
            blocks_of(first_ref, 0, TOGETHER * group, TOGETHER),
            group,
            begin * BLOCK,
        )
        scores = jnp.where(allowed, scores, floor_score)
        peak = jnp.max(scores, axis=0, keepdims=True)
        mass = jnp.exp2(scores - peak)
        total = jnp.sum(mass, axis=0, keepdims=True)
        mass_ref[pl.ds(group, 1), :] = peak + jnp.log2(total)
        prob = (mass * (1.0 / total)).astype(bf16)
        value_grad_s[rows, :] += dot(prob, blocks_of(first_ref, 2, TOGETHER * group, TOGETHER))

    by_window(info_ref, chunks, window)
    half = info_ref[info_ref.shape[0] - 1]
    for c in range(chunks // 2):
        low = value_grad_s[block_rows(c), :]
        high = value_grad_s[block_rows(chunks // 2 + c), :]
        kept_ref[block_rows(c), :] = jnp.where(half == 0, low, high)
        sent_ref[block_rows(c), :] = jnp.where(half == 0, high, low).astype(bf16)


def softmax_grads(
    features, info_ref, first_ref, mass_ref, raw_ref, other_ref, sums_ref, other_sums_ref, out_ref,
    key_t_s, value_s, value_t_s, key_grad_s,
):
    chunks, width = (first_ref.shape[0], first_ref.shape[2])
    side = chunks // 2
    scale = 1.0 / math.sqrt(width)
    half = info_ref[info_ref.shape[0] - 1]
    inverse, other_inverse = [
        (1.0 / jnp.sqrt(ref[0:side, :] / features + norm_epsilon)).T for ref in (sums_ref, other_sums_ref)
    ]
    for c in range(chunks):
        here = block_rows(c)
        there = block_rows(c % side)
        own = jnp.where(half == 0, raw_ref[0, there, :], raw_ref[1, there, :])
        own = own.astype(f32) * column(inverse, c % side)
        other = other_ref[there, :].astype(f32) * column(other_inverse, c % side)
        v = jnp.where(half == c // side, own, other).astype(bf16)
        value_s[here, :] = v
        value_t_s[:, here] = v.T
        key_t_s[:, here] = first_ref[c, BLOCK : 2 * BLOCK, :].T
        key_grad_s[here, :] = jnp.zeros((BLOCK, width), f32)

    def window(group, begin, blocks):
        rows = pl.ds(pl.multiple_of(begin * BLOCK, 2 * BLOCK), blocks * BLOCK)
        queries = blocks_of(first_ref, 0, TOGETHER * group, TOGETHER)
        keys = blocks_of(first_ref, 1, begin, blocks)
        scores, allowed = window_scores(info_ref, keys, queries, group, begin * BLOCK)
        scores = jnp.where(allowed, scores - mass_ref[pl.ds(group, 1), :], floor_score)
        prob = jnp.exp2(scores)
        g_t = blocks_of(first_ref, 2, TOGETHER * group, TOGETHER).T
        attended = dot(value_t_s[:, rows], prob.astype(bf16))
        delta = jnp.sum(g_t.astype(f32) * attended, axis=0, keepdims=True)
        grad_prob = dot(value_s[rows, :], g_t)
        grad_score = (prob * ((grad_prob - delta) * scale)).astype(bf16)
        key_grad_s[rows, :] += dot(grad_score, queries)
        query_grad = dot(key_t_s[:, rows], grad_score).T.astype(bf16)
        for c in range(TOGETHER):
            out_ref[TOGETHER * group + c, 0:BLOCK, :] = query_grad[block_rows(c), :]

    by_window(info_ref, chunks, window)
    for c in range(chunks):
        out_ref[c, BLOCK : 2 * BLOCK, :] = key_grad_s[block_rows(c), :].astype(bf16)


def call(kernel, micros, outs, scratch, *operands, prefetch=0, room=8, whole=False):
    vmem = pl.BlockSpec(memory_space=pltpu.VMEM)
    smem = pl.BlockSpec(memory_space=pltpu.SMEM)
    results = [jax.ShapeDtypeStruct(shape, kind) for shape, kind in outs]
    held = [jax.ShapeDtypeStruct(shape, kind) for shape, kind in scratch]
    size = sum(
        a.size * a.dtype.itemsize for a in [*held, *(([*operands, *results]) if whole else [])]
    )
    return pl.pallas_call(
        kernel,
        out_shape=results,
        in_specs=[smem] * prefetch + [vmem] * (len(operands) - prefetch),
        out_specs=[vmem] * len(outs),
        scratch_shapes=[pltpu.VMEM(shape, kind) for shape, kind in scratch],
        compiler_params=pltpu.CompilerParams(vmem_limit_bytes=size + room * 1024 * 1024),
        cost_estimate=pl.CostEstimate(
            flops=int(micros * 1e9), bytes_accessed=int(micros * 3e6), transcendentals=0
        ),
    )(*operands)


def swap_matrix(chunks):
    size = chunks * chunks
    i = lax.broadcasted_iota(jnp.int32, (size, size), 0)
    j = lax.broadcasted_iota(jnp.int32, (size, size), 1)
    return jnp.where(j == (i % chunks) * chunks + i // chunks, 1.0, 0.0).astype(bf16)


def pair_order(heads):
    return [(h % 2) * (heads // 2) + h // 2 for h in range(heads)]


def pack(order, *refs):
    arrays, out_ref = ([ref for ref in refs[:-1] if len(ref.shape) == 3], refs[-1])
    length, heads, width = arrays[0].shape
    swap = swap_matrix(heads)
    for place, ref in enumerate(arrays):
        for begin in range(0, length, heads):
            rows = ref[begin : begin + heads].reshape(heads * heads, width)
            swapped = dot(swap, rows).astype(bf16)
            row = place * length + begin
            for h in range(heads):
                out_ref[order[h], row : row + heads, :] = swapped[h * heads : (h + 1) * heads, :]
    if len(arrays) == len(refs) - 1:
        return
    decay_ref = refs[-2]
    high, _ = two_parts(decay_ref[...])
    middle, last = two_parts(decay_ref[...] - high.astype(f32))
    row = lax.broadcasted_iota(jnp.int32, (PART_ROWS, length), 0)
    for h in range(heads):
        tile = jnp.zeros((PART_ROWS, length), f32)
        for n, part in enumerate((high, middle, last)):
            tile = jnp.where(row == n, part[h : h + 1, :].astype(f32), tile)
        out_ref[order[h], len(arrays) * length :, :] = tile.astype(bf16)


def unpack(order, in_ref, *outs):
    length, heads, width = outs[0].shape
    swap = swap_matrix(heads)
    for place, out_ref in enumerate(outs):
        for begin in range(0, length, heads):
            row = place * length + begin
            rows = jnp.concatenate(
                [in_ref[order[h], row : row + heads, :] for h in range(heads)], axis=0
            )
            out_ref[begin : begin + heads] = dot(swap, rows).reshape(heads, heads, width)


def exchange(x):
    return lax.all_to_all(x, "seq", 0, 0, tiled=True)


def exchange_half(x):
    side = lax.axis_size("seq") // 2
    groups = [list(range(side)), list(range(side, 2 * side))]
    return lax.all_to_all(x, "seq", 0, 0, tiled=True, axis_index_groups=groups)


def upward(x):
    side = lax.axis_size("seq") // 2
    return lax.ppermute(x, "seq", [(i, i + side) for i in range(side)])


def downward(x):
    side = lax.axis_size("seq") // 2
    return lax.ppermute(x, "seq", [(i + side, i) for i in range(side)])


def swapped(x):
    side = lax.axis_size("seq") // 2
    return lax.ppermute(x, "seq", [(i, (i + side) % (2 * side)) for i in range(2 * side)])


def over_heads(mine):
    count = lax.axis_size("head")
    total = mine
    for step in range(1, count):
        total = total + lax.ppermute(mine, "head", [(i, (i + step) % count) for i in range(count)])
    return total


def body(query_one, key_one, value_one, log_decay, query_two, key_two, out_grad, doc_ids):
    length, heads_here, width = query_one.shape
    shards = lax.axis_size("seq")
    if heads_here != shards or length != BLOCK or shards != 16 or width != BLOCK:
        return ring_body(
            query_one, key_one, value_one, log_decay, query_two, key_two, out_grad, doc_ids
        )
    side = shards // 2
    heads = heads_here // side
    half_length = side * length
    features = heads_here * lax.axis_size("head") * width
    half = (lax.axis_index("seq") >= side).astype(jnp.int32)
    starts = jnp.sum((doc_ids[None, :] < doc_ids[:, None]).astype(jnp.int32), axis=1)
    info = jnp.concatenate([starts, half[None]])
    straight, paired = (list(range(heads_here)), pair_order(heads_here))

    def packed(order, rows, arrays, *more):
        arrays = [pltpu.with_memory_space_constraint(array, pltpu.HBM) for array in arrays]
        return call(
            partial(pack, order), 3, [((heads_here, rows, width), bf16)], [], *arrays, *more, whole=True
        )[0]

    first = exchange(packed(paired, 3 * length, (query_two, key_two, out_grad)))
    second = packed(straight, 3 * length + PART_ROWS, (query_one, key_one, value_one), log_decay)
    second, first = lax.optimization_barrier((second, first))
    second = exchange_half(second)
    half_rows = (half_length, width)
    full_rows = (shards * length, width)
    masses, grad_kept, grad_sent = call(
        softmax_masses,
        6,
        [
            ((shards // TOGETHER, GROUP), f32),
            (half_rows, f32),
            (half_rows, bf16),
        ],
        [(full_rows, f32)],
        info,
        first,
        prefetch=1,
    )
    grad_other = swapped(grad_sent)
    state_shape = (heads, width, width)
    (state,) = call(partial(linear_state, heads), 1, [(state_shape, f32)], [], second)
    incoming = upward(state)
    head_rows = (heads, half_length, width)
    (local,) = call(partial(linear_local, heads), 4, [(head_rows, f32)], [], second)
    raw, raw_sent, sums = call(
        partial(linear_output, heads),
        2,
        [(head_rows, bf16), (half_rows, bf16), ((2 * side, BLOCK), f32)],
        [],
        info,
        second,
        incoming,
        local,
        grad_kept,
        grad_other,
        prefetch=1,
    )
    raw_other = swapped(raw_sent)
    sums = exchange_half(jnp.broadcast_to(sums[None], (side,) + sums.shape))
    sums = over_heads(jnp.sum(sums, axis=0))
    sums_other = swapped(sums[:side])
    (softmax_grad,) = call(
        partial(softmax_grads, features),
        7,
        [((shards, 2 * BLOCK, width), bf16)],
        [
            ((width, shards * length), bf16),
            (full_rows, bf16),
            ((width, shards * length), bf16),
            (full_rows, f32),
        ],
        info,
        first,
        masses,
        raw,
        raw_other,
        sums,
        sums_other,
        prefetch=1,
    )
    (state_grad,) = call(
        partial(linear_state_grad, features, heads),
        2,
        [(state_shape, f32)],
        [],
        info,
        second,
        raw,
        sums,
        grad_kept,
        grad_other,
        prefetch=1,
    )
    later_grad = downward(state_grad)
    later_grad, softmax_grad = lax.optimization_barrier((later_grad, softmax_grad))
    softmax_grad = exchange(softmax_grad)
    (linear_grads,) = call(
        partial(linear_backward, features, heads),
        5,
        [((heads_here, 3 * BLOCK, width), bf16)],
        [((heads, side, width, width), bf16)],
        info,
        second,
        raw,
        incoming,
        sums,
        grad_kept,
        grad_other,
        later_grad,
        prefetch=1,
    )
    softmax_grad, linear_grads = lax.optimization_barrier((softmax_grad, linear_grads))
    linear_grads = exchange_half(linear_grads)

    def unpacked(order, count, received):
        outs = [((length, heads_here, width), f32)] * count
        return call(partial(unpack, order), count, outs, [], received, whole=True)

    query_one_grad, key_one_grad, value_one_grad = unpacked(straight, 3, linear_grads)
    query_two_grad, key_two_grad = unpacked(paired, 2, softmax_grad)
    return (query_one_grad, key_one_grad, value_one_grad, query_two_grad, key_two_grad)


def solution(mesh):
    placed = (
        P("seq", "head", None),
        P("seq", "head", None),
        P("seq", "head", None),
        P("head", "seq"),
        P("seq", "head", None),
        P("seq", "head", None),
        P("seq", "head", None),
        P(),
    )
    return jax.shard_map(
        body,
        mesh=mesh,
        in_specs=placed,
        out_specs=(P("seq", "head", None),) * 5,
        check_vma=False,
    )
```

```python
from functools import partial
import math

import jax
import jax.numpy as jnp
from jax import lax
from jax.experimental import pallas as pl
from jax.experimental.pallas import tpu as pltpu
from jax.sharding import PartitionSpec as P

BLOCK = 128
REACH = 8


exact_precision = lax.Precision.HIGHEST
floor_score = -1e30
norm_epsilon = 1e-05


def prefix(value, axis, join, neutral, backward):
    count, mine = (lax.axis_size(axis), lax.axis_index(axis))
    pieces = jax.tree.map(lambda part: lax.all_gather(part, axis), value)
    if backward:
        pieces = jax.tree.map(lambda part: part[::-1], pieces)
        mine = count - 1 - mine
    total = jax.tree.map(
        lambda part, zero: jnp.full_like(part, 0) + jnp.asarray(zero, part.dtype), value, neutral
    )

    def hop(position, total):
        longer = join(total, jax.tree.map(lambda part: part[position], pieces))
        return jax.tree.map(lambda new, old: jnp.where(position < mine, new, old), longer, total)

    return lax.fori_loop(0, count - 1, hop, total)


def from_behind(block, axis, distance):
    devices = range(lax.axis_size(axis))
    route = [(i - distance, i) for i in devices if i - distance in devices]
    return lax.ppermute(block, axis, route)


def for_sending(shard):
    return jax.tree.map(lambda a: a.astype(jnp.bfloat16) if a.dtype == jnp.float32 else a, shard)


def lower_mask(length):
    return lax.broadcasted_iota(jnp.int32, (length, length), 0) >= lax.broadcasted_iota(
        jnp.int32, (length, length), 1
    )


def shard_output(q_float, k_float, v_float, cumulative, incoming):
    lower = lower_mask(q_float.shape[0])[None]
    gaps = cumulative[:, :, None] - cumulative[:, None, :]
    weights = jnp.where(lower, jnp.exp(jnp.where(lower, gaps, 0.0)), 0.0)
    scores = jnp.einsum("thd,uhd->htu", q_float, k_float, precision=exact_precision) * weights
    inner_part = jnp.einsum("htu,uhe->the", scores, v_float, precision=exact_precision)
    outer_part = jnp.einsum(
        "thd,hde->the",
        q_float * jnp.exp(cumulative).T[:, :, None],
        incoming,
        precision=exact_precision,
    )
    return inner_part + outer_part


def shard_state(k_float, v_float, cumulative):
    tail_decay = jnp.exp(cumulative[:, -1:] - cumulative)
    return jnp.einsum(
        "uhd,uhe->hde", k_float * tail_decay.T[:, :, None], v_float, precision=exact_precision
    )


def chain_join(earlier, later):
    return (earlier[0] * later[0], later[0][:, None, None] * earlier[1] + later[1])


def scores_work(query_two, keys_block, allowed, scale):
    raw_scores = (
        jnp.einsum("thd,uhd->htu", query_two, keys_block, preferred_element_type=jnp.float32)
        * scale
    )
    return jnp.where(allowed[None], raw_scores, floor_score)


def probs_work(tile_scores, log_mass, allowed, values_block):
    prob = jnp.where(allowed[None], jnp.exp(tile_scores - log_mass[:, :, None]), 0.0)
    part_out = jnp.einsum(
        "htu,uhd->thd", prob.astype(jnp.bfloat16), values_block, preferred_element_type=jnp.float32
    )
    return (prob, part_out)


def grads_work(prob, query_two, out_grad, keys_block, values_block, delta, scale):
    grad_prob = jnp.einsum(
        "thd,uhd->htu", out_grad, values_block, preferred_element_type=jnp.float32
    )
    grad_score = (prob * (grad_prob - delta.T[:, :, None]) * scale).astype(jnp.bfloat16)
    query_grad = jnp.einsum(
        "htu,uhd->thd", grad_score, keys_block, preferred_element_type=jnp.float32
    )
    key_grad = jnp.einsum("htu,thd->uhd", grad_score, query_two, preferred_element_type=jnp.float32)
    value_grad = jnp.einsum(
        "htu,thd->uhd", prob.astype(jnp.bfloat16), out_grad, preferred_element_type=jnp.float32
    )
    return (query_grad, key_grad, value_grad)


def ring_body(query_one, key_one, value_one, log_decay, query_two, key_two, out_grad, doc_ids):
    length, heads_here, width = query_one.shape
    shards = lax.axis_size("seq")
    token_position = lax.axis_index("seq")
    features = heads_here * lax.axis_size("head") * width
    q_float = query_one.astype(jnp.float32)
    k_float = key_one.astype(jnp.float32)
    v_float = value_one.astype(jnp.float32)
    cumulative = jnp.cumsum(log_decay, axis=1)
    carry_decay = jnp.exp(cumulative[:, -1])
    local_state, state_pull = jax.vjp(partial(shard_state, cumulative=cumulative), k_float, v_float)
    identity = (jnp.ones_like(carry_decay), jnp.zeros_like(local_state))
    incoming = prefix((carry_decay, local_state), "seq", chain_join, identity, False)[1]
    raw_out, output_pull = jax.vjp(
        partial(shard_output, cumulative=cumulative, incoming=incoming), q_float, k_float, v_float
    )
    square_sum = lax.psum(jnp.sum(raw_out * raw_out, axis=(1, 2)), "head")
    inverse = 1.0 / jnp.sqrt(square_sum / features + norm_epsilon)
    normed = raw_out * inverse[:, None, None]
    values_two = normed.astype(jnp.bfloat16)
    blocks_here = length // BLOCK
    scale = 1.0 / math.sqrt(width)
    offsets = jnp.arange(length, dtype=jnp.int32)
    query_doc = jnp.repeat(
        lax.dynamic_slice_in_dim(doc_ids, token_position * blocks_here, blocks_here), BLOCK
    )
    query_pos = token_position * length + offsets
    masks = []
    for distance in range(REACH + 1):
        source = (token_position - distance) % shards
        key_doc = jnp.repeat(
            lax.dynamic_slice_in_dim(doc_ids, source * blocks_here, blocks_here), BLOCK
        )
        key_pos = source * length + offsets
        masks.append(
            (key_pos[None, :] <= query_pos[:, None]) & (key_doc[None, :] == query_doc[:, None])
        )
    blocks = [(key_two, values_two)]
    current = (key_two, values_two)
    for distance in range(1, REACH + 1):
        current = from_behind((current[0], current[1]), "seq", 1)
        blocks.append(current)
    row_shape = (length, heads_here, width)
    peak_now = jnp.full((heads_here, length), floor_score, jnp.float32)
    mass_now = jnp.zeros((heads_here, length), jnp.float32)
    tile_list = []
    for distance in range(REACH + 1):
        allowed = masks[distance]
        tile_scores = scores_work(query_two, blocks[distance][0], allowed, scale)
        peak_next = jnp.maximum(peak_now, jnp.max(tile_scores, axis=2))
        fresh_mass = jnp.sum(
            jnp.where(allowed[None], jnp.exp(tile_scores - peak_next[:, :, None]), 0.0), axis=2
        )
        mass_now = mass_now * jnp.exp(peak_now - peak_next) + fresh_mass
        peak_now = peak_next
        tile_list.append(tile_scores)
    log_mass = peak_now + jnp.log(mass_now)
    attended = jnp.zeros(row_shape, jnp.float32)
    prob_list = []
    for distance in range(REACH + 1):
        allowed = masks[distance]
        prob, part_out = probs_work(tile_list[distance], log_mass, allowed, blocks[distance][1])
        attended = attended + part_out
        prob_list.append(prob)
    delta = jnp.sum(out_grad.astype(jnp.float32) * attended, axis=2)
    grad_query_two = jnp.zeros(row_shape, jnp.float32)
    carried = None
    for distance in range(REACH, -1, -1):
        keys_block, values_block = blocks[distance]
        query_grad, key_grad, value_grad = grads_work(
            prob_list[distance], query_two, out_grad, keys_block, values_block, delta, scale
        )
        grad_query_two = grad_query_two + query_grad
        if carried is None:
            carried = (key_grad, value_grad)
        else:
            moved = jax.tree.map(
                lambda part, own: part.astype(own.dtype),
                from_behind(for_sending(carried), "seq", -1),
                carried,
            )
            carried = (moved[0] + key_grad, moved[1] + value_grad)
    grad_key_two, grad_values_two = carried
    cross_sum = lax.psum(jnp.sum(raw_out * grad_values_two, axis=(1, 2)), "head")
    grad_raw = (
        inverse[:, None, None] * grad_values_two
        - raw_out * (inverse**3 * cross_sum / features)[:, None, None]
    )
    direct_state = jnp.einsum(
        "thd,the->hde",
        q_float * jnp.exp(cumulative).T[:, :, None],
        grad_raw,
        precision=exact_precision,
    )
    later_grad = prefix((carry_decay, direct_state), "seq", chain_join, identity, True)[1]
    grad_query_one, grad_key_out, grad_value_out = output_pull(grad_raw)
    grad_key_state, grad_value_state = state_pull(later_grad)
    return (
        grad_query_one,
        grad_key_out + grad_key_state,
        grad_value_out + grad_value_state,
        grad_query_two,
        grad_key_two,
    )


f32, bf16 = (jnp.float32, jnp.bfloat16)
LOG2E = math.log2(math.e)
PART_ROWS = 16


def dot(a, b):
    return lax.dot_general(a, b, (((1,), (0,)), ((), ())), preferred_element_type=f32)


def dot_nt(a, b):
    return lax.dot_general(a, b, (((1,), (1,)), ((), ())), preferred_element_type=f32)


def dot_tn(a, b):
    return lax.dot_general(a, b, (((0,), (0,)), ((), ())), preferred_element_type=f32)


def two_parts(value):
    high = value.astype(bf16)
    return high, (value - high.astype(f32)).astype(bf16)


def row_sums(value):
    ones = jnp.ones((PART_ROWS, value.shape[1]), bf16)
    high, low = two_parts(value)
    return dot_nt(ones, high) + dot_nt(ones, low)


def decay_column(parts):
    log_row = jnp.sum(parts.astype(f32), axis=0, keepdims=True)
    return jnp.sum(jnp.where(lower_mask(BLOCK), log_row, 0.0), axis=1, keepdims=True)


def chunk_decays(parts):
    lower = lower_mask(BLOCK)
    column = decay_column(parts)
    upper = lax.broadcasted_iota(jnp.int32, (BLOCK, BLOCK), 0) <= lax.broadcasted_iota(
        jnp.int32, (BLOCK, BLOCK), 1
    )
    row = jnp.sum(dot(parts, jnp.where(upper, 1.0, 0.0).astype(bf16)), axis=0, keepdims=True)
    last = column[BLOCK - 1 : BLOCK, :]
    weights = jnp.exp(jnp.where(lower, column - row, floor_score))
    return weights, jnp.exp(column), jnp.exp(last - column), jnp.exp(last)


def lightning_piece(ref, place):
    arrays = [ref[place, n * BLOCK : (n + 1) * BLOCK, :] for n in range(3)]
    return arrays + [chunk_decays(ref[place, ref.shape[1] - PART_ROWS :, :])]


UNROLL = 16


def over_chunks(chunks, body, carry, backward=False):
    unrolled = math.gcd(UNROLL, chunks)

    def step(n, carry):
        for part in range(unrolled):
            c = n * unrolled + part
            carry = body(chunks - 1 - c if backward else c, carry)
        return carry

    if unrolled == chunks:
        return step(0, carry)
    return lax.fori_loop(0, chunks // unrolled, step, carry)


def block_rows(c):
    if isinstance(c, int):
        return slice(c * BLOCK, (c + 1) * BLOCK)
    return pl.ds(pl.multiple_of(c * BLOCK, BLOCK), BLOCK)


def linear_state(heads, second_ref, state_ref):
    chunks, width = (second_ref.shape[0] // heads, second_ref.shape[2])

    def chunk(c, states):
        following = []
        for head in range(heads):
            _, k, v, (_, _, tail, whole) = lightning_piece(second_ref, c * heads + head)
            following.append(
                whole * states[head] + dot_tn(k, (v.astype(f32) * tail).astype(bf16))
            )
        return tuple(following)

    states = over_chunks(chunks, chunk, (jnp.zeros((width, width), f32),) * heads)
    for head in range(heads):
        state_ref[head] = states[head]


def value_gradient(half, kept_ref, other_ref, head, c):
    return jnp.where(
        half == head, kept_ref[block_rows(c), :], other_ref[block_rows(c), :].astype(f32)
    )


def linear_local(heads, second_ref, raw_ref):
    chunks, width = (second_ref.shape[0] // heads, second_ref.shape[2])

    def chunk(c, states):
        following = []
        for head in range(heads):
            q, k, v, (weights, grow, tail, whole) = lightning_piece(second_ref, c * heads + head)
            prob = (dot_nt(q, k) * weights).astype(bf16)
            raw = dot(prob, v) + grow * dot(q, states[head].astype(bf16))
            raw_ref[head, block_rows(c), :] = raw
            following.append(
                whole * states[head] + dot_tn(k, (v.astype(f32) * tail).astype(bf16))
            )
        return tuple(following)

    over_chunks(chunks, chunk, (jnp.zeros((width, width), f32),) * heads)


def linear_output(
    heads, info_ref, second_ref, incoming_ref, local_ref, kept_ref, other_ref, raw_ref, sent_ref, sums_ref
):
    chunks = second_ref.shape[0] // heads
    half = info_ref[info_ref.shape[0] - 1]
    incoming = [incoming_ref[head].astype(bf16) for head in range(heads)]
    carried = [jnp.ones((1, 1), f32)] * heads
    columns = jnp.zeros((BLOCK, BLOCK), f32)
    lanes = lax.broadcasted_iota(jnp.int32, (BLOCK, BLOCK), 1)
    for c in range(chunks):
        here = block_rows(c)
        raws = []
        squares, products = (0.0, 0.0)
        for head in range(heads):
            place = c * heads + head
            logs = decay_column(second_ref[place, second_ref.shape[1] - PART_ROWS :, :])
            outer = dot(second_ref[place, 0:BLOCK, :], incoming[head])
            raw = local_ref[head, here, :] + (carried[head] * jnp.exp(logs)) * outer
            carried[head] = carried[head] * jnp.exp(logs[BLOCK - 1 : BLOCK, :])
            grad = value_gradient(half, kept_ref, other_ref, head, c)
            squares = squares + raw * raw
            products = products + raw * grad
            raws.append(raw.astype(bf16))
            raw_ref[head, here, :] = raws[head]
        sent_ref[here, :] = jnp.where(half == 0, raws[1], raws[0])
        for place, part in ((c, squares), (chunks + c, products)):
            total = jnp.sum(part, axis=1, keepdims=True)
            columns = jnp.where(lanes == place, total, columns)
    sums_ref[...] = columns.T[0 : 2 * chunks, :]


def column(columns, c):
    if isinstance(c, int):
        return columns[:, c : c + 1]
    lanes = lax.broadcasted_iota(jnp.int32, columns.shape, 1)
    return jnp.sum(jnp.where(lanes == c, columns, 0.0), axis=1, keepdims=True)


def norm_columns(features, sums_ref):
    chunks = sums_ref.shape[0] // 2
    inverse = 1.0 / jnp.sqrt(sums_ref[0:chunks, :] / features + norm_epsilon)
    return inverse.T, (inverse * inverse * inverse * sums_ref[chunks:, :] / features).T


def linear_state_grad(
    features, heads, info_ref, second_ref, raw_ref, sums_ref, kept_ref, other_ref, state_grad_ref
):
    chunks, width = (second_ref.shape[0] // heads, second_ref.shape[2])
    half = info_ref[info_ref.shape[0] - 1]
    inverse, cross = norm_columns(features, sums_ref)

    def chunk(c, grads):
        following = []
        for head in range(heads):
            q, _, _, (_, grow, _, whole) = lightning_piece(second_ref, c * heads + head)
            grad = column(inverse, c) * value_gradient(half, kept_ref, other_ref, head, c)
            grad = grad - raw_ref[head, block_rows(c), :].astype(f32) * column(cross, c)
            following.append(whole * grads[head] + dot_tn(q, (grad * grow).astype(bf16)))
        return tuple(following)

    grads = over_chunks(chunks, chunk, (jnp.zeros((width, width), f32),) * heads, True)
    for head in range(heads):
        state_grad_ref[head] = grads[head]


def linear_backward(
    features, heads, info_ref, second_ref, raw_ref, incoming_ref, sums_ref, kept_ref, other_ref, later_ref,
    out_ref, state_s,
):
    chunks = second_ref.shape[0] // heads

    def before(c, states):
        following = []
        for head in range(heads):
            _, k, v, (_, _, tail, whole) = lightning_piece(second_ref, c * heads + head)
            state_s[head, c] = states[head].astype(bf16)
            following.append(
                whole * states[head] + dot_tn(k, (v.astype(f32) * tail).astype(bf16))
            )
        return tuple(following)

    over_chunks(chunks, before, tuple(incoming_ref[head] for head in range(heads)))
    half = info_ref[info_ref.shape[0] - 1]
    inverse, cross = norm_columns(features, sums_ref)

    def chunk(c, grads):
        following = []
        for head in range(heads):
            place = c * heads + head
            q, k, v, (weights, grow, tail, whole) = lightning_piece(second_ref, place)
            grad = column(inverse, c) * value_gradient(half, kept_ref, other_ref, head, c)
            grad = grad - raw_ref[head, block_rows(c), :].astype(f32) * column(cross, c)
            grad_low = grad.astype(bf16)
            prob = (dot_nt(q, k) * weights).astype(bf16)
            grad_score = (dot_nt(grad_low, v) * weights).astype(bf16)
            state_low = grads[head].astype(bf16)
            query_grad = dot(grad_score, k) + grow * dot_nt(grad_low, state_s[head, c])
            key_grad = dot_tn(grad_score, q) + tail * dot_nt(v, state_low)
            value_grad = dot_tn(prob, grad_low) + tail * dot(k, state_low)
            following.append(whole * grads[head] + dot_tn(q, (grad * grow).astype(bf16)))
            out_ref[place, 0:BLOCK, :] = query_grad.astype(bf16)
            out_ref[place, BLOCK : 2 * BLOCK, :] = key_grad.astype(bf16)
            out_ref[place, 2 * BLOCK : 3 * BLOCK, :] = value_grad.astype(bf16)
        return tuple(following)

    over_chunks(chunks, chunk, tuple(later_ref[head] for head in range(heads)), True)


TOGETHER = 4
GROUP = TOGETHER * BLOCK


def by_window(info_ref, chunks, window):
    def step(group, carry):
        end = TOGETHER * (group + 1)
        need = end - info_ref[TOGETHER * group]
        least = 0
        for blocks in window_sizes(chunks):
            begin = end - blocks
            pl.when((need > least) & (need <= blocks))(partial(window, group, begin, blocks))
            least = blocks
        return carry

    lax.fori_loop(0, chunks // TOGETHER, step, 0)


def window_sizes(chunks):
    return range(TOGETHER, min(chunks, REACH + TOGETHER) + 1, 2)


def window_scores(info_ref, keys, queries, group, begin):
    shape = (keys.shape[0], queries.shape[0])
    scores = dot(keys, queries.T) * (LOG2E / math.sqrt(keys.shape[1]))
    u_pos = begin + lax.broadcasted_iota(jnp.int32, shape, 0)
    lane = lax.broadcasted_iota(jnp.int32, (1, shape[1]), 1)
    lowest = jnp.zeros_like(lane)
    for n in range(TOGETHER):
        lowest = jnp.where(lane >= n * BLOCK, info_ref[TOGETHER * group + n] * BLOCK, lowest)
    return scores, (u_pos >= lowest) & (u_pos <= group * GROUP + lane)


def blocks_of(first_ref, place, block, count):
    rows = first_ref[pl.ds(block, count), place * BLOCK : (place + 1) * BLOCK, :]
    return rows.reshape(count * BLOCK, first_ref.shape[2])


def softmax_masses(info_ref, first_ref, mass_ref, kept_ref, sent_ref, value_grad_s):
    chunks, width = (first_ref.shape[0], first_ref.shape[2])
    value_grad_s[...] = jnp.zeros_like(value_grad_s)

    def window(group, begin, blocks):
        rows = pl.ds(pl.multiple_of(begin * BLOCK, 2 * BLOCK), blocks * BLOCK)
        scores, allowed = window_scores(
            info_ref,
            blocks_of(first_ref, 1, begin, blocks),
            blocks_of(first_ref, 0, TOGETHER * group, TOGETHER),
            group,
            begin * BLOCK,
        )
        scores = jnp.where(allowed, scores, floor_score)
        peak = jnp.max(scores, axis=0, keepdims=True)
        mass = jnp.exp2(scores - peak)
        total = jnp.sum(mass, axis=0, keepdims=True)
        mass_ref[pl.ds(group, 1), :] = peak + jnp.log2(total)
        prob = (mass * (1.0 / total)).astype(bf16)
        value_grad_s[rows, :] += dot(prob, blocks_of(first_ref, 2, TOGETHER * group, TOGETHER))

    by_window(info_ref, chunks, window)
    half = info_ref[info_ref.shape[0] - 1]
    for c in range(chunks // 2):
        low = value_grad_s[block_rows(c), :]
        high = value_grad_s[block_rows(chunks // 2 + c), :]
        kept_ref[block_rows(c), :] = jnp.where(half == 0, low, high)
        sent_ref[block_rows(c), :] = jnp.where(half == 0, high, low).astype(bf16)


def softmax_grads(
    features, info_ref, first_ref, mass_ref, raw_ref, other_ref, sums_ref, other_sums_ref, out_ref,
    key_t_s, value_s, value_t_s, key_grad_s,
):
    chunks, width = (first_ref.shape[0], first_ref.shape[2])
    side = chunks // 2
    scale = 1.0 / math.sqrt(width)
    half = info_ref[info_ref.shape[0] - 1]
    inverse, other_inverse = [
        (1.0 / jnp.sqrt(ref[0:side, :] / features + norm_epsilon)).T for ref in (sums_ref, other_sums_ref)
    ]
    for c in range(chunks):
        here = block_rows(c)
        there = block_rows(c % side)
        own = jnp.where(half == 0, raw_ref[0, there, :], raw_ref[1, there, :])
        own = own.astype(f32) * column(inverse, c % side)
        other = other_ref[there, :].astype(f32) * column(other_inverse, c % side)
        v = jnp.where(half == c // side, own, other).astype(bf16)
        value_s[here, :] = v
        value_t_s[:, here] = v.T
        key_t_s[:, here] = first_ref[c, BLOCK : 2 * BLOCK, :].T
        key_grad_s[here, :] = jnp.zeros((BLOCK, width), f32)

    def window(group, begin, blocks):
        rows = pl.ds(pl.multiple_of(begin * BLOCK, 2 * BLOCK), blocks * BLOCK)
        queries = blocks_of(first_ref, 0, TOGETHER * group, TOGETHER)
        keys = blocks_of(first_ref, 1, begin, blocks)
        scores, allowed = window_scores(info_ref, keys, queries, group, begin * BLOCK)
        scores = jnp.where(allowed, scores - mass_ref[pl.ds(group, 1), :], floor_score)
        prob = jnp.exp2(scores)
        g_t = blocks_of(first_ref, 2, TOGETHER * group, TOGETHER).T
        attended = dot(value_t_s[:, rows], prob.astype(bf16))
        delta = jnp.sum(g_t.astype(f32) * attended, axis=0, keepdims=True)
        grad_prob = dot(value_s[rows, :], g_t)
        grad_score = (prob * ((grad_prob - delta) * scale)).astype(bf16)
        key_grad_s[rows, :] += dot(grad_score, queries)
        query_grad = dot(key_t_s[:, rows], grad_score).T.astype(bf16)
        for c in range(TOGETHER):
            out_ref[TOGETHER * group + c, 0:BLOCK, :] = query_grad[block_rows(c), :]

    by_window(info_ref, chunks, window)
    for c in range(chunks):
        out_ref[c, BLOCK : 2 * BLOCK, :] = key_grad_s[block_rows(c), :].astype(bf16)


def call(kernel, micros, outs, scratch, *operands, prefetch=0, room=8, whole=False):
    vmem = pl.BlockSpec(memory_space=pltpu.VMEM)
    smem = pl.BlockSpec(memory_space=pltpu.SMEM)
    results = [jax.ShapeDtypeStruct(shape, kind) for shape, kind in outs]
    held = [jax.ShapeDtypeStruct(shape, kind) for shape, kind in scratch]
    size = sum(
        a.size * a.dtype.itemsize for a in [*held, *(([*operands, *results]) if whole else [])]
    )
    return pl.pallas_call(
        kernel,
        out_shape=results,
        in_specs=[smem] * prefetch + [vmem] * (len(operands) - prefetch),
        out_specs=[vmem] * len(outs),
        scratch_shapes=[pltpu.VMEM(shape, kind) for shape, kind in scratch],
        compiler_params=pltpu.CompilerParams(vmem_limit_bytes=size + room * 1024 * 1024),
        cost_estimate=pl.CostEstimate(
            flops=int(micros * 1e9), bytes_accessed=int(micros * 3e6), transcendentals=0
        ),
    )(*operands)


def swap_matrix(chunks):
    size = chunks * chunks
    i = lax.broadcasted_iota(jnp.int32, (size, size), 0)
    j = lax.broadcasted_iota(jnp.int32, (size, size), 1)
    return jnp.where(j == (i % chunks) * chunks + i // chunks, 1.0, 0.0).astype(bf16)


def pair_order(heads):
    return [(h % 2) * (heads // 2) + h // 2 for h in range(heads)]


def pack(order, *refs):
    arrays, out_ref = ([ref for ref in refs[:-1] if len(ref.shape) == 3], refs[-1])
    length, heads, width = arrays[0].shape
    swap = swap_matrix(heads)
    for place, ref in enumerate(arrays):
        for begin in range(0, length, heads):
            rows = ref[begin : begin + heads].reshape(heads * heads, width)
            swapped = dot(swap, rows).astype(bf16)
            row = place * length + begin
            for h in range(heads):
                out_ref[order[h], row : row + heads, :] = swapped[h * heads : (h + 1) * heads, :]
    if len(arrays) == len(refs) - 1:
        return
    decay_ref = refs[-2]
    high, _ = two_parts(decay_ref[...])
    middle, last = two_parts(decay_ref[...] - high.astype(f32))
    row = lax.broadcasted_iota(jnp.int32, (PART_ROWS, length), 0)
    for h in range(heads):
        tile = jnp.zeros((PART_ROWS, length), f32)
        for n, part in enumerate((high, middle, last)):
            tile = jnp.where(row == n, part[h : h + 1, :].astype(f32), tile)
        out_ref[order[h], len(arrays) * length :, :] = tile.astype(bf16)


def unpack(order, in_ref, *outs):
    length, heads, width = outs[0].shape
    swap = swap_matrix(heads)
    for place, out_ref in enumerate(outs):
        for begin in range(0, length, heads):
            row = place * length + begin
            rows = jnp.concatenate(
                [in_ref[order[h], row : row + heads, :] for h in range(heads)], axis=0
            )
            out_ref[begin : begin + heads] = dot(swap, rows).reshape(heads, heads, width)


def exchange(x):
    return lax.all_to_all(x, "seq", 0, 0, tiled=True)


def exchange_half(x):
    side = lax.axis_size("seq") // 2
    groups = [list(range(side)), list(range(side, 2 * side))]
    return lax.all_to_all(x, "seq", 0, 0, tiled=True, axis_index_groups=groups)


def upward(x):
    side = lax.axis_size("seq") // 2
    return lax.ppermute(x, "seq", [(i, i + side) for i in range(side)])


def downward(x):
    side = lax.axis_size("seq") // 2
    return lax.ppermute(x, "seq", [(i + side, i) for i in range(side)])


def swapped(x):
    side = lax.axis_size("seq") // 2
    return lax.ppermute(x, "seq", [(i, (i + side) % (2 * side)) for i in range(2 * side)])


def over_heads(mine):
    count = lax.axis_size("head")
    total = mine
    for step in range(1, count):
        total = total + lax.ppermute(mine, "head", [(i, (i + step) % count) for i in range(count)])
    return total


def body(query_one, key_one, value_one, log_decay, query_two, key_two, out_grad, doc_ids):
    length, heads_here, width = query_one.shape
    shards = lax.axis_size("seq")
    if heads_here != shards or length != BLOCK or shards != 16 or width != BLOCK:
        return ring_body(
            query_one, key_one, value_one, log_decay, query_two, key_two, out_grad, doc_ids
        )
    side = shards // 2
    heads = heads_here // side
    half_length = side * length
    features = heads_here * lax.axis_size("head") * width
    half = (lax.axis_index("seq") >= side).astype(jnp.int32)
    starts = jnp.sum((doc_ids[None, :] < doc_ids[:, None]).astype(jnp.int32), axis=1)
    info = jnp.concatenate([starts, half[None]])
    straight, paired = (list(range(heads_here)), pair_order(heads_here))

    def packed(order, rows, arrays, *more):
        arrays = [pltpu.with_memory_space_constraint(array, pltpu.HBM) for array in arrays]
        return call(
            partial(pack, order), 3, [((heads_here, rows, width), bf16)], [], *arrays, *more, whole=True
        )[0]

    first = exchange(packed(paired, 3 * length, (query_two, key_two, out_grad)))
    second = packed(straight, 3 * length + PART_ROWS, (query_one, key_one, value_one), log_decay)
    second, first = lax.optimization_barrier((second, first))
    second = exchange_half(second)
    half_rows = (half_length, width)
    full_rows = (shards * length, width)
    masses, grad_kept, grad_sent = call(
        softmax_masses,
        6,
        [
            ((shards // TOGETHER, GROUP), f32),
            (half_rows, f32),
            (half_rows, bf16),
        ],
        [(full_rows, f32)],
        info,
        first,
        prefetch=1,
    )
    grad_other = swapped(grad_sent)
    state_shape = (heads, width, width)
    (state,) = call(partial(linear_state, heads), 1, [(state_shape, f32)], [], second)
    incoming = upward(state)
    head_rows = (heads, half_length, width)
    (local,) = call(partial(linear_local, heads), 4, [(head_rows, f32)], [], second)
    raw, raw_sent, sums = call(
        partial(linear_output, heads),
        2,
        [(head_rows, bf16), (half_rows, bf16), ((2 * side, BLOCK), f32)],
        [],
        info,
        second,
        incoming,
        local,
        grad_kept,
        grad_other,
        prefetch=1,
    )
    raw_other = swapped(raw_sent)
    sums = exchange_half(jnp.broadcast_to(sums[None], (side,) + sums.shape))
    sums = over_heads(jnp.sum(sums, axis=0))
    sums_other = swapped(sums[:side])
    (softmax_grad,) = call(
        partial(softmax_grads, features),
        7,
        [((shards, 2 * BLOCK, width), bf16)],
        [
            ((width, shards * length), bf16),
            (full_rows, bf16),
            ((width, shards * length), bf16),
            (full_rows, f32),
        ],
        info,
        first,
        masses,
        raw,
        raw_other,
        sums,
        sums_other,
        prefetch=1,
    )
    (state_grad,) = call(
        partial(linear_state_grad, features, heads),
        2,
        [(state_shape, f32)],
        [],
        info,
        second,
        raw,
        sums,
        grad_kept,
        grad_other,
        prefetch=1,
    )
    later_grad = downward(state_grad)
    later_grad, softmax_grad = lax.optimization_barrier((later_grad, softmax_grad))
    softmax_grad = exchange(softmax_grad)
    (linear_grads,) = call(
        partial(linear_backward, features, heads),
        5,
        [((heads_here, 3 * BLOCK, width), bf16)],
        [((heads, side, width, width), bf16)],
        info,
        second,
        raw,
        incoming,
        sums,
        grad_kept,
        grad_other,
        later_grad,
        prefetch=1,
    )
    softmax_grad, linear_grads = lax.optimization_barrier((softmax_grad, linear_grads))
    linear_grads = exchange_half(linear_grads)

    def unpacked(order, count, received):
        outs = [((length, heads_here, width), f32)] * count
        return call(partial(unpack, order), count, outs, [], received, whole=True)

    query_one_grad, key_one_grad, value_one_grad = unpacked(straight, 3, linear_grads)
    query_two_grad, key_two_grad = unpacked(paired, 2, softmax_grad)
    return (query_one_grad, key_one_grad, value_one_grad, query_two_grad, key_two_grad)


def solution(mesh):
    placed = (
        P("seq", "head", None),
        P("seq", "head", None),
        P("seq", "head", None),
        P("head", "seq"),
        P("seq", "head", None),
        P("seq", "head", None),
        P("seq", "head", None),
        P(),
    )
    return jax.shard_map(
        body,
        mesh=mesh,
        in_specs=placed,
        out_specs=(P("seq", "head", None),) * 5,
        check_vma=False,
    )
```

```python
from functools import partial
import math

import jax
import jax.numpy as jnp
from jax import lax
from jax.experimental import pallas as pl
from jax.experimental.pallas import tpu as pltpu
from jax.sharding import PartitionSpec as P

BLOCK = 128
REACH = 8


exact_precision = lax.Precision.HIGHEST
floor_score = -1e30
norm_epsilon = 1e-05


def prefix(value, axis, join, neutral, backward):
    count, mine = (lax.axis_size(axis), lax.axis_index(axis))
    pieces = jax.tree.map(lambda part: lax.all_gather(part, axis), value)
    if backward:
        pieces = jax.tree.map(lambda part: part[::-1], pieces)
        mine = count - 1 - mine
    total = jax.tree.map(
        lambda part, zero: jnp.full_like(part, 0) + jnp.asarray(zero, part.dtype), value, neutral
    )

    def hop(position, total):
        longer = join(total, jax.tree.map(lambda part: part[position], pieces))
        return jax.tree.map(lambda new, old: jnp.where(position < mine, new, old), longer, total)

    return lax.fori_loop(0, count - 1, hop, total)


def from_behind(block, axis, distance):
    devices = range(lax.axis_size(axis))
    route = [(i - distance, i) for i in devices if i - distance in devices]
    return lax.ppermute(block, axis, route)


def for_sending(shard):
    return jax.tree.map(lambda a: a.astype(jnp.bfloat16) if a.dtype == jnp.float32 else a, shard)


def lower_mask(length):
    return lax.broadcasted_iota(jnp.int32, (length, length), 0) >= lax.broadcasted_iota(
        jnp.int32, (length, length), 1
    )


def shard_output(q_float, k_float, v_float, cumulative, incoming):
    lower = lower_mask(q_float.shape[0])[None]
    gaps = cumulative[:, :, None] - cumulative[:, None, :]
    weights = jnp.where(lower, jnp.exp(jnp.where(lower, gaps, 0.0)), 0.0)
    scores = jnp.einsum("thd,uhd->htu", q_float, k_float, precision=exact_precision) * weights
    inner_part = jnp.einsum("htu,uhe->the", scores, v_float, precision=exact_precision)
    outer_part = jnp.einsum(
        "thd,hde->the",
        q_float * jnp.exp(cumulative).T[:, :, None],
        incoming,
        precision=exact_precision,
    )
    return inner_part + outer_part


def shard_state(k_float, v_float, cumulative):
    tail_decay = jnp.exp(cumulative[:, -1:] - cumulative)
    return jnp.einsum(
        "uhd,uhe->hde", k_float * tail_decay.T[:, :, None], v_float, precision=exact_precision
    )


def chain_join(earlier, later):
    return (earlier[0] * later[0], later[0][:, None, None] * earlier[1] + later[1])


def scores_work(query_two, keys_block, allowed, scale):
    raw_scores = (
        jnp.einsum("thd,uhd->htu", query_two, keys_block, preferred_element_type=jnp.float32)
        * scale
    )
    return jnp.where(allowed[None], raw_scores, floor_score)


def probs_work(tile_scores, log_mass, allowed, values_block):
    prob = jnp.where(allowed[None], jnp.exp(tile_scores - log_mass[:, :, None]), 0.0)
    part_out = jnp.einsum(
        "htu,uhd->thd", prob.astype(jnp.bfloat16), values_block, preferred_element_type=jnp.float32
    )
    return (prob, part_out)


def grads_work(prob, query_two, out_grad, keys_block, values_block, delta, scale):
    grad_prob = jnp.einsum(
        "thd,uhd->htu", out_grad, values_block, preferred_element_type=jnp.float32
    )
    grad_score = (prob * (grad_prob - delta.T[:, :, None]) * scale).astype(jnp.bfloat16)
    query_grad = jnp.einsum(
        "htu,uhd->thd", grad_score, keys_block, preferred_element_type=jnp.float32
    )
    key_grad = jnp.einsum("htu,thd->uhd", grad_score, query_two, preferred_element_type=jnp.float32)
    value_grad = jnp.einsum(
        "htu,thd->uhd", prob.astype(jnp.bfloat16), out_grad, preferred_element_type=jnp.float32
    )
    return (query_grad, key_grad, value_grad)


def ring_body(query_one, key_one, value_one, log_decay, query_two, key_two, out_grad, doc_ids):
    length, heads_here, width = query_one.shape
    shards = lax.axis_size("seq")
    token_position = lax.axis_index("seq")
    features = heads_here * lax.axis_size("head") * width
    q_float = query_one.astype(jnp.float32)
    k_float = key_one.astype(jnp.float32)
    v_float = value_one.astype(jnp.float32)
    cumulative = jnp.cumsum(log_decay, axis=1)
    carry_decay = jnp.exp(cumulative[:, -1])
    local_state, state_pull = jax.vjp(partial(shard_state, cumulative=cumulative), k_float, v_float)
    identity = (jnp.ones_like(carry_decay), jnp.zeros_like(local_state))
    incoming = prefix((carry_decay, local_state), "seq", chain_join, identity, False)[1]
    raw_out, output_pull = jax.vjp(
        partial(shard_output, cumulative=cumulative, incoming=incoming), q_float, k_float, v_float
    )
    square_sum = lax.psum(jnp.sum(raw_out * raw_out, axis=(1, 2)), "head")
    inverse = 1.0 / jnp.sqrt(square_sum / features + norm_epsilon)
    normed = raw_out * inverse[:, None, None]
    values_two = normed.astype(jnp.bfloat16)
    blocks_here = length // BLOCK
    scale = 1.0 / math.sqrt(width)
    offsets = jnp.arange(length, dtype=jnp.int32)
    query_doc = jnp.repeat(
        lax.dynamic_slice_in_dim(doc_ids, token_position * blocks_here, blocks_here), BLOCK
    )
    query_pos = token_position * length + offsets
    masks = []
    for distance in range(REACH + 1):
        source = (token_position - distance) % shards
        key_doc = jnp.repeat(
            lax.dynamic_slice_in_dim(doc_ids, source * blocks_here, blocks_here), BLOCK
        )
        key_pos = source * length + offsets
        masks.append(
            (key_pos[None, :] <= query_pos[:, None]) & (key_doc[None, :] == query_doc[:, None])
        )
    blocks = [(key_two, values_two)]
    current = (key_two, values_two)
    for distance in range(1, REACH + 1):
        current = from_behind((current[0], current[1]), "seq", 1)
        blocks.append(current)
    row_shape = (length, heads_here, width)
    peak_now = jnp.full((heads_here, length), floor_score, jnp.float32)
    mass_now = jnp.zeros((heads_here, length), jnp.float32)
    tile_list = []
    for distance in range(REACH + 1):
        allowed = masks[distance]
        tile_scores = scores_work(query_two, blocks[distance][0], allowed, scale)
        peak_next = jnp.maximum(peak_now, jnp.max(tile_scores, axis=2))
        fresh_mass = jnp.sum(
            jnp.where(allowed[None], jnp.exp(tile_scores - peak_next[:, :, None]), 0.0), axis=2
        )
        mass_now = mass_now * jnp.exp(peak_now - peak_next) + fresh_mass
        peak_now = peak_next
        tile_list.append(tile_scores)
    log_mass = peak_now + jnp.log(mass_now)
    attended = jnp.zeros(row_shape, jnp.float32)
    prob_list = []
    for distance in range(REACH + 1):
        allowed = masks[distance]
        prob, part_out = probs_work(tile_list[distance], log_mass, allowed, blocks[distance][1])
        attended = attended + part_out
        prob_list.append(prob)
    delta = jnp.sum(out_grad.astype(jnp.float32) * attended, axis=2)
    grad_query_two = jnp.zeros(row_shape, jnp.float32)
    carried = None
    for distance in range(REACH, -1, -1):
        keys_block, values_block = blocks[distance]
        query_grad, key_grad, value_grad = grads_work(
            prob_list[distance], query_two, out_grad, keys_block, values_block, delta, scale
        )
        grad_query_two = grad_query_two + query_grad
        if carried is None:
            carried = (key_grad, value_grad)
        else:
            moved = jax.tree.map(
                lambda part, own: part.astype(own.dtype),
                from_behind(for_sending(carried), "seq", -1),
                carried,
            )
            carried = (moved[0] + key_grad, moved[1] + value_grad)
    grad_key_two, grad_values_two = carried
    cross_sum = lax.psum(jnp.sum(raw_out * grad_values_two, axis=(1, 2)), "head")
    grad_raw = (
        inverse[:, None, None] * grad_values_two
        - raw_out * (inverse**3 * cross_sum / features)[:, None, None]
    )
    direct_state = jnp.einsum(
        "thd,the->hde",
        q_float * jnp.exp(cumulative).T[:, :, None],
        grad_raw,
        precision=exact_precision,
    )
    later_grad = prefix((carry_decay, direct_state), "seq", chain_join, identity, True)[1]
    grad_query_one, grad_key_out, grad_value_out = output_pull(grad_raw)
    grad_key_state, grad_value_state = state_pull(later_grad)
    return (
        grad_query_one,
        grad_key_out + grad_key_state,
        grad_value_out + grad_value_state,
        grad_query_two,
        grad_key_two,
    )


f32, bf16 = (jnp.float32, jnp.bfloat16)
LOG2E = math.log2(math.e)
PART_ROWS = 16


def dot(a, b):
    return lax.dot_general(a, b, (((1,), (0,)), ((), ())), preferred_element_type=f32)


def dot_nt(a, b):
    return lax.dot_general(a, b, (((1,), (1,)), ((), ())), preferred_element_type=f32)


def dot_tn(a, b):
    return lax.dot_general(a, b, (((0,), (0,)), ((), ())), preferred_element_type=f32)


def two_parts(value):
    high = value.astype(bf16)
    return high, (value - high.astype(f32)).astype(bf16)


def row_sums(value):
    ones = jnp.ones((PART_ROWS, value.shape[1]), bf16)
    high, low = two_parts(value)
    return dot_nt(ones, high) + dot_nt(ones, low)


def decay_column(parts):
    log_row = jnp.sum(parts.astype(f32), axis=0, keepdims=True)
    return jnp.sum(jnp.where(lower_mask(BLOCK), log_row, 0.0), axis=1, keepdims=True)


def chunk_decays(parts):
    lower = lower_mask(BLOCK)
    column = decay_column(parts)
    upper = lax.broadcasted_iota(jnp.int32, (BLOCK, BLOCK), 0) <= lax.broadcasted_iota(
        jnp.int32, (BLOCK, BLOCK), 1
    )
    row = jnp.sum(dot(parts, jnp.where(upper, 1.0, 0.0).astype(bf16)), axis=0, keepdims=True)
    last = column[BLOCK - 1 : BLOCK, :]
    weights = jnp.exp(jnp.where(lower, column - row, floor_score))
    return weights, jnp.exp(column), jnp.exp(last - column), jnp.exp(last)


def lightning_piece(ref, place):
    arrays = [ref[place, n * BLOCK : (n + 1) * BLOCK, :] for n in range(3)]
    return arrays + [chunk_decays(ref[place, ref.shape[1] - PART_ROWS :, :])]


UNROLL = 16


def over_chunks(chunks, body, carry, backward=False):
    unrolled = math.gcd(UNROLL, chunks)

    def step(n, carry):
        for part in range(unrolled):
            c = n * unrolled + part
            carry = body(chunks - 1 - c if backward else c, carry)
        return carry

    if unrolled == chunks:
        return step(0, carry)
    return lax.fori_loop(0, chunks // unrolled, step, carry)


def block_rows(c):
    if isinstance(c, int):
        return slice(c * BLOCK, (c + 1) * BLOCK)
    return pl.ds(pl.multiple_of(c * BLOCK, BLOCK), BLOCK)


def linear_state(heads, second_ref, state_ref):
    chunks, width = (second_ref.shape[0] // heads, second_ref.shape[2])

    def chunk(c, states):
        following = []
        for head in range(heads):
            _, k, v, (_, _, tail, whole) = lightning_piece(second_ref, c * heads + head)
            following.append(
                whole * states[head] + dot_tn(k, (v.astype(f32) * tail).astype(bf16))
            )
        return tuple(following)

    states = over_chunks(chunks, chunk, (jnp.zeros((width, width), f32),) * heads)
    for head in range(heads):
        state_ref[head] = states[head]


def value_gradient(half, kept_ref, other_ref, head, c):
    return jnp.where(
        half == head, kept_ref[block_rows(c), :], other_ref[block_rows(c), :].astype(f32)
    )


def linear_local(heads, second_ref, raw_ref):
    chunks, width = (second_ref.shape[0] // heads, second_ref.shape[2])

    def chunk(c, states):
        following = []
        for head in range(heads):
            q, k, v, (weights, grow, tail, whole) = lightning_piece(second_ref, c * heads + head)
            prob = (dot_nt(q, k) * weights).astype(bf16)
            raw = dot(prob, v) + grow * dot(q, states[head].astype(bf16))
            raw_ref[head, block_rows(c), :] = raw
            following.append(
                whole * states[head] + dot_tn(k, (v.astype(f32) * tail).astype(bf16))
            )
        return tuple(following)

    over_chunks(chunks, chunk, (jnp.zeros((width, width), f32),) * heads)


def linear_output(
    heads, info_ref, second_ref, incoming_ref, local_ref, kept_ref, other_ref, raw_ref, sent_ref, sums_ref
):
    chunks = second_ref.shape[0] // heads
    half = info_ref[info_ref.shape[0] - 1]
    incoming = [incoming_ref[head].astype(bf16) for head in range(heads)]
    carried = [jnp.ones((1, 1), f32)] * heads
    columns = jnp.zeros((BLOCK, BLOCK), f32)
    lanes = lax.broadcasted_iota(jnp.int32, (BLOCK, BLOCK), 1)
    for c in range(chunks):
        here = block_rows(c)
        raws = []
        squares, products = (0.0, 0.0)
        for head in range(heads):
            place = c * heads + head
            logs = decay_column(second_ref[place, second_ref.shape[1] - PART_ROWS :, :])
            outer = dot(second_ref[place, 0:BLOCK, :], incoming[head])
            raw = local_ref[head, here, :] + (carried[head] * jnp.exp(logs)) * outer
            carried[head] = carried[head] * jnp.exp(logs[BLOCK - 1 : BLOCK, :])
            grad = value_gradient(half, kept_ref, other_ref, head, c)
            squares = squares + raw * raw
            products = products + raw * grad
            raws.append(raw.astype(bf16))
            raw_ref[head, here, :] = raws[head]
        sent_ref[here, :] = jnp.where(half == 0, raws[1], raws[0])
        for place, part in ((c, squares), (chunks + c, products)):
            total = jnp.sum(part, axis=1, keepdims=True)
            columns = jnp.where(lanes == place, total, columns)
    sums_ref[...] = columns.T[0 : 2 * chunks, :]


def column(columns, c):
    if isinstance(c, int):
        return columns[:, c : c + 1]
    lanes = lax.broadcasted_iota(jnp.int32, columns.shape, 1)
    return jnp.sum(jnp.where(lanes == c, columns, 0.0), axis=1, keepdims=True)


def norm_columns(features, sums_ref):
    chunks = sums_ref.shape[0] // 2
    inverse = 1.0 / jnp.sqrt(sums_ref[0:chunks, :] / features + norm_epsilon)
    return inverse.T, (inverse * inverse * inverse * sums_ref[chunks:, :] / features).T


def linear_state_grad(
    features, heads, info_ref, second_ref, raw_ref, sums_ref, kept_ref, other_ref, state_grad_ref
):
    chunks, width = (second_ref.shape[0] // heads, second_ref.shape[2])
    half = info_ref[info_ref.shape[0] - 1]
    inverse, cross = norm_columns(features, sums_ref)

    def chunk(c, grads):
        following = []
        for head in range(heads):
            q, _, _, (_, grow, _, whole) = lightning_piece(second_ref, c * heads + head)
            grad = column(inverse, c) * value_gradient(half, kept_ref, other_ref, head, c)
            grad = grad - raw_ref[head, block_rows(c), :].astype(f32) * column(cross, c)
            following.append(whole * grads[head] + dot_tn(q, (grad * grow).astype(bf16)))
        return tuple(following)

    grads = over_chunks(chunks, chunk, (jnp.zeros((width, width), f32),) * heads, True)
    for head in range(heads):
        state_grad_ref[head] = grads[head]


def linear_backward(
    features, heads, info_ref, second_ref, raw_ref, incoming_ref, sums_ref, kept_ref, other_ref, later_ref,
    out_ref, state_s,
):
    chunks = second_ref.shape[0] // heads

    def before(c, states):
        following = []
        for head in range(heads):
            _, k, v, (_, _, tail, whole) = lightning_piece(second_ref, c * heads + head)
            state_s[head, c] = states[head].astype(bf16)
            following.append(
                whole * states[head] + dot_tn(k, (v.astype(f32) * tail).astype(bf16))
            )
        return tuple(following)

    over_chunks(chunks, before, tuple(incoming_ref[head] for head in range(heads)))
    half = info_ref[info_ref.shape[0] - 1]
    inverse, cross = norm_columns(features, sums_ref)

    def chunk(c, grads):
        following = []
        for head in range(heads):
            place = c * heads + head
            q, k, v, (weights, grow, tail, whole) = lightning_piece(second_ref, place)
            grad = column(inverse, c) * value_gradient(half, kept_ref, other_ref, head, c)
            grad = grad - raw_ref[head, block_rows(c), :].astype(f32) * column(cross, c)
            grad_low = grad.astype(bf16)
            prob = (dot_nt(q, k) * weights).astype(bf16)
            grad_score = (dot_nt(grad_low, v) * weights).astype(bf16)
            state_low = grads[head].astype(bf16)
            query_grad = dot(grad_score, k) + grow * dot_nt(grad_low, state_s[head, c])
            key_grad = dot_tn(grad_score, q) + tail * dot_nt(v, state_low)
            value_grad = dot_tn(prob, grad_low) + tail * dot(k, state_low)
            following.append(whole * grads[head] + dot_tn(q, (grad * grow).astype(bf16)))
            out_ref[place, 0:BLOCK, :] = query_grad.astype(bf16)
            out_ref[place, BLOCK : 2 * BLOCK, :] = key_grad.astype(bf16)
            out_ref[place, 2 * BLOCK : 3 * BLOCK, :] = value_grad.astype(bf16)
        return tuple(following)

    over_chunks(chunks, chunk, tuple(later_ref[head] for head in range(heads)), True)


TOGETHER = 4
GROUP = TOGETHER * BLOCK


def by_window(info_ref, chunks, window):
    def step(group, carry):
        end = TOGETHER * (group + 1)
        need = end - info_ref[TOGETHER * group]
        least = 0
        for blocks in window_sizes(chunks):
            begin = end - blocks
            pl.when((need > least) & (need <= blocks))(partial(window, group, begin, blocks))
            least = blocks
        return carry

    lax.fori_loop(0, chunks // TOGETHER, step, 0)


def window_sizes(chunks):
    return range(TOGETHER, min(chunks, REACH + TOGETHER) + 1, 2)


def window_scores(info_ref, keys, queries, group, begin):
    shape = (keys.shape[0], queries.shape[0])
    scores = dot(keys, queries.T) * (LOG2E / math.sqrt(keys.shape[1]))
    u_pos = begin + lax.broadcasted_iota(jnp.int32, shape, 0)
    lane = lax.broadcasted_iota(jnp.int32, (1, shape[1]), 1)
    lowest = jnp.zeros_like(lane)
    for n in range(TOGETHER):
        lowest = jnp.where(lane >= n * BLOCK, info_ref[TOGETHER * group + n] * BLOCK, lowest)
    return scores, (u_pos >= lowest) & (u_pos <= group * GROUP + lane)


def blocks_of(first_ref, place, block, count):
    rows = first_ref[pl.ds(block, count), place * BLOCK : (place + 1) * BLOCK, :]
    return rows.reshape(count * BLOCK, first_ref.shape[2])


def softmax_masses(info_ref, first_ref, mass_ref, kept_ref, sent_ref, value_grad_s):
    chunks, width = (first_ref.shape[0], first_ref.shape[2])
    value_grad_s[...] = jnp.zeros_like(value_grad_s)

    def window(group, begin, blocks):
        rows = pl.ds(pl.multiple_of(begin * BLOCK, 2 * BLOCK), blocks * BLOCK)
        scores, allowed = window_scores(
            info_ref,
            blocks_of(first_ref, 1, begin, blocks),
            blocks_of(first_ref, 0, TOGETHER * group, TOGETHER),
            group,
            begin * BLOCK,
        )
        scores = jnp.where(allowed, scores, floor_score)
        peak = jnp.max(scores, axis=0, keepdims=True)
        mass = jnp.exp2(scores - peak)
        total = jnp.sum(mass, axis=0, keepdims=True)
        mass_ref[pl.ds(group, 1), :] = peak + jnp.log2(total)
        prob = (mass * (1.0 / total)).astype(bf16)
        value_grad_s[rows, :] += dot(prob, blocks_of(first_ref, 2, TOGETHER * group, TOGETHER))

    by_window(info_ref, chunks, window)
    half = info_ref[info_ref.shape[0] - 1]
    for c in range(chunks // 2):
        low = value_grad_s[block_rows(c), :]
        high = value_grad_s[block_rows(chunks // 2 + c), :]
        kept_ref[block_rows(c), :] = jnp.where(half == 0, low, high)
        sent_ref[block_rows(c), :] = jnp.where(half == 0, high, low).astype(bf16)


def softmax_grads(
    features, info_ref, first_ref, mass_ref, raw_ref, other_ref, sums_ref, other_sums_ref, out_ref,
    key_t_s, value_s, value_t_s, key_grad_s,
):
    chunks, width = (first_ref.shape[0], first_ref.shape[2])
    side = chunks // 2
    scale = 1.0 / math.sqrt(width)
    half = info_ref[info_ref.shape[0] - 1]
    inverse, other_inverse = [
        (1.0 / jnp.sqrt(ref[0:side, :] / features + norm_epsilon)).T for ref in (sums_ref, other_sums_ref)
    ]
    for c in range(chunks):
        here = block_rows(c)
        there = block_rows(c % side)
        own = jnp.where(half == 0, raw_ref[0, there, :], raw_ref[1, there, :])
        own = own.astype(f32) * column(inverse, c % side)
        other = other_ref[there, :].astype(f32) * column(other_inverse, c % side)
        v = jnp.where(half == c // side, own, other).astype(bf16)
        value_s[here, :] = v
        value_t_s[:, here] = v.T
        key_t_s[:, here] = first_ref[c, BLOCK : 2 * BLOCK, :].T
        key_grad_s[here, :] = jnp.zeros((BLOCK, width), f32)

    def window(group, begin, blocks):
        rows = pl.ds(pl.multiple_of(begin * BLOCK, 2 * BLOCK), blocks * BLOCK)
        queries = blocks_of(first_ref, 0, TOGETHER * group, TOGETHER)
        keys = blocks_of(first_ref, 1, begin, blocks)
        scores, allowed = window_scores(info_ref, keys, queries, group, begin * BLOCK)
        scores = jnp.where(allowed, scores - mass_ref[pl.ds(group, 1), :], floor_score)
        prob = jnp.exp2(scores)
        g_t = blocks_of(first_ref, 2, TOGETHER * group, TOGETHER).T
        attended = dot(value_t_s[:, rows], prob.astype(bf16))
        delta = jnp.sum(g_t.astype(f32) * attended, axis=0, keepdims=True)
        grad_prob = dot(value_s[rows, :], g_t)
        grad_score = (prob * ((grad_prob - delta) * scale)).astype(bf16)
        key_grad_s[rows, :] += dot(grad_score, queries)
        query_grad = dot(key_t_s[:, rows], grad_score).T.astype(bf16)
        for c in range(TOGETHER):
            out_ref[TOGETHER * group + c, 0:BLOCK, :] = query_grad[block_rows(c), :]

    by_window(info_ref, chunks, window)
    for c in range(chunks):
        out_ref[c, BLOCK : 2 * BLOCK, :] = key_grad_s[block_rows(c), :].astype(bf16)


def call(kernel, micros, outs, scratch, *operands, prefetch=0, room=8, whole=False):
    vmem = pl.BlockSpec(memory_space=pltpu.VMEM)
    smem = pl.BlockSpec(memory_space=pltpu.SMEM)
    results = [jax.ShapeDtypeStruct(shape, kind) for shape, kind in outs]
    held = [jax.ShapeDtypeStruct(shape, kind) for shape, kind in scratch]
    size = sum(
        a.size * a.dtype.itemsize for a in [*held, *(([*operands, *results]) if whole else [])]
    )
    return pl.pallas_call(
        kernel,
        out_shape=results,
        in_specs=[smem] * prefetch + [vmem] * (len(operands) - prefetch),
        out_specs=[vmem] * len(outs),
        scratch_shapes=[pltpu.VMEM(shape, kind) for shape, kind in scratch],
        compiler_params=pltpu.CompilerParams(vmem_limit_bytes=size + room * 1024 * 1024),
        cost_estimate=pl.CostEstimate(
            flops=int(micros * 1e9), bytes_accessed=int(micros * 3e6), transcendentals=0
        ),
    )(*operands)


def swap_matrix(chunks):
    size = chunks * chunks
    i = lax.broadcasted_iota(jnp.int32, (size, size), 0)
    j = lax.broadcasted_iota(jnp.int32, (size, size), 1)
    return jnp.where(j == (i % chunks) * chunks + i // chunks, 1.0, 0.0).astype(bf16)


def pair_order(heads):
    return [(h % 2) * (heads // 2) + h // 2 for h in range(heads)]


def pack(order, *refs):
    arrays, out_ref = ([ref for ref in refs[:-1] if len(ref.shape) == 3], refs[-1])
    length, heads, width = arrays[0].shape
    swap = swap_matrix(heads)
    for place, ref in enumerate(arrays):
        for begin in range(0, length, heads):
            rows = ref[begin : begin + heads].reshape(heads * heads, width)
            swapped = dot(swap, rows).astype(bf16)
            row = place * length + begin
            for h in range(heads):
                out_ref[order[h], row : row + heads, :] = swapped[h * heads : (h + 1) * heads, :]
    if len(arrays) == len(refs) - 1:
        return
    decay_ref = refs[-2]
    high, _ = two_parts(decay_ref[...])
    middle, last = two_parts(decay_ref[...] - high.astype(f32))
    row = lax.broadcasted_iota(jnp.int32, (PART_ROWS, length), 0)
    for h in range(heads):
        tile = jnp.zeros((PART_ROWS, length), f32)
        for n, part in enumerate((high, middle, last)):
            tile = jnp.where(row == n, part[h : h + 1, :].astype(f32), tile)
        out_ref[order[h], len(arrays) * length :, :] = tile.astype(bf16)


def unpack(order, in_ref, *outs):
    length, heads, width = outs[0].shape
    swap = swap_matrix(heads)
    for place, out_ref in enumerate(outs):
        for begin in range(0, length, heads):
            row = place * length + begin
            rows = jnp.concatenate(
                [in_ref[order[h], row : row + heads, :] for h in range(heads)], axis=0
            )
            out_ref[begin : begin + heads] = dot(swap, rows).reshape(heads, heads, width)


def exchange(x):
    return lax.all_to_all(x, "seq", 0, 0, tiled=True)


def exchange_half(x):
    side = lax.axis_size("seq") // 2
    groups = [list(range(side)), list(range(side, 2 * side))]
    return lax.all_to_all(x, "seq", 0, 0, tiled=True, axis_index_groups=groups)


def upward(x):
    side = lax.axis_size("seq") // 2
    return lax.ppermute(x, "seq", [(i, i + side) for i in range(side)])


def downward(x):
    side = lax.axis_size("seq") // 2
    return lax.ppermute(x, "seq", [(i + side, i) for i in range(side)])


def swapped(x):
    side = lax.axis_size("seq") // 2
    return lax.ppermute(x, "seq", [(i, (i + side) % (2 * side)) for i in range(2 * side)])


def over_heads(mine):
    count = lax.axis_size("head")
    total = mine
    for step in range(1, count):
        total = total + lax.ppermute(mine, "head", [(i, (i + step) % count) for i in range(count)])
    return total


def body(query_one, key_one, value_one, log_decay, query_two, key_two, out_grad, doc_ids):
    length, heads_here, width = query_one.shape
    shards = lax.axis_size("seq")
    if heads_here != shards or length != BLOCK or shards != 16 or width != BLOCK:
        return ring_body(
            query_one, key_one, value_one, log_decay, query_two, key_two, out_grad, doc_ids
        )
    side = shards // 2
    heads = heads_here // side
    half_length = side * length
    features = heads_here * lax.axis_size("head") * width
    half = (lax.axis_index("seq") >= side).astype(jnp.int32)
    starts = jnp.sum((doc_ids[None, :] < doc_ids[:, None]).astype(jnp.int32), axis=1)
    info = jnp.concatenate([starts, half[None]])
    straight, paired = (list(range(heads_here)), pair_order(heads_here))

    def packed(order, rows, arrays, *more):
        arrays = [pltpu.with_memory_space_constraint(array, pltpu.HBM) for array in arrays]
        return call(
            partial(pack, order), 3, [((heads_here, rows, width), bf16)], [], *arrays, *more, whole=True
        )[0]

    first = exchange(packed(paired, 3 * length, (query_two, key_two, out_grad)))
    second = packed(straight, 3 * length + PART_ROWS, (query_one, key_one, value_one), log_decay)
    second, first = lax.optimization_barrier((second, first))
    second = exchange_half(second)
    half_rows = (half_length, width)
    full_rows = (shards * length, width)
    masses, grad_kept, grad_sent = call(
        softmax_masses,
        6,
        [
            ((shards // TOGETHER, GROUP), f32),
            (half_rows, f32),
            (half_rows, bf16),
        ],
        [(full_rows, f32)],
        info,
        first,
        prefetch=1,
    )
    grad_other = swapped(grad_sent)
    state_shape = (heads, width, width)
    (state,) = call(partial(linear_state, heads), 1, [(state_shape, f32)], [], second)
    incoming = upward(state)
    head_rows = (heads, half_length, width)
    (local,) = call(partial(linear_local, heads), 4, [(head_rows, f32)], [], second)
    raw, raw_sent, sums = call(
        partial(linear_output, heads),
        2,
        [(head_rows, bf16), (half_rows, bf16), ((2 * side, BLOCK), f32)],
        [],
        info,
        second,
        incoming,
        local,
        grad_kept,
        grad_other,
        prefetch=1,
    )
    raw_other = swapped(raw_sent)
    sums = exchange_half(jnp.broadcast_to(sums[None], (side,) + sums.shape))
    sums = over_heads(jnp.sum(sums, axis=0))
    sums_other = swapped(sums[:side])
    (softmax_grad,) = call(
        partial(softmax_grads, features),
        7,
        [((shards, 2 * BLOCK, width), bf16)],
        [
            ((width, shards * length), bf16),
            (full_rows, bf16),
            ((width, shards * length), bf16),
            (full_rows, f32),
        ],
        info,
        first,
        masses,
        raw,
        raw_other,
        sums,
        sums_other,
        prefetch=1,
    )
    raw_in_hbm = pltpu.with_memory_space_constraint(raw, pltpu.HBM)
    kept_in_hbm = pltpu.with_memory_space_constraint(grad_kept, pltpu.HBM)
    (state_grad,) = call(
        partial(linear_state_grad, features, heads),
        2,
        [(state_shape, f32)],
        [],
        info,
        second,
        raw_in_hbm,
        sums,
        kept_in_hbm,
        grad_other,
        prefetch=1,
    )
    later_grad = downward(state_grad)
    later_grad, softmax_grad = lax.optimization_barrier((later_grad, softmax_grad))
    softmax_grad = exchange(softmax_grad)
    (linear_grads,) = call(
        partial(linear_backward, features, heads),
        5,
        [((heads_here, 3 * BLOCK, width), bf16)],
        [((heads, side, width, width), bf16)],
        info,
        second,
        raw_in_hbm,
        incoming,
        sums,
        kept_in_hbm,
        grad_other,
        later_grad,
        prefetch=1,
    )
    softmax_grad, linear_grads = lax.optimization_barrier((softmax_grad, linear_grads))
    linear_grads = exchange_half(linear_grads)

    def unpacked(order, count, received):
        outs = [((length, heads_here, width), f32)] * count
        return call(partial(unpack, order), count, outs, [], received, whole=True)

    query_one_grad, key_one_grad, value_one_grad = unpacked(straight, 3, linear_grads)
    query_two_grad, key_two_grad = unpacked(paired, 2, softmax_grad)
    return (query_one_grad, key_one_grad, value_one_grad, query_two_grad, key_two_grad)


def solution(mesh):
    placed = (
        P("seq", "head", None),
        P("seq", "head", None),
        P("seq", "head", None),
        P("head", "seq"),
        P("seq", "head", None),
        P("seq", "head", None),
        P("seq", "head", None),
        P(),
    )
    return jax.shard_map(
        body,
        mesh=mesh,
        in_specs=placed,
        out_specs=(P("seq", "head", None),) * 5,
        check_vma=False,
    )
```

```python
from functools import partial
import math

import jax
import jax.numpy as jnp
from jax import lax
from jax.experimental import pallas as pl
from jax.experimental.pallas import tpu as pltpu
from jax.sharding import PartitionSpec as P

BLOCK = 128
REACH = 8


exact_precision = lax.Precision.HIGHEST
floor_score = -1e30
norm_epsilon = 1e-05


def prefix(value, axis, join, neutral, backward):
    count, mine = (lax.axis_size(axis), lax.axis_index(axis))
    pieces = jax.tree.map(lambda part: lax.all_gather(part, axis), value)
    if backward:
        pieces = jax.tree.map(lambda part: part[::-1], pieces)
        mine = count - 1 - mine
    total = jax.tree.map(
        lambda part, zero: jnp.full_like(part, 0) + jnp.asarray(zero, part.dtype), value, neutral
    )

    def hop(position, total):
        longer = join(total, jax.tree.map(lambda part: part[position], pieces))
        return jax.tree.map(lambda new, old: jnp.where(position < mine, new, old), longer, total)

    return lax.fori_loop(0, count - 1, hop, total)


def from_behind(block, axis, distance):
    devices = range(lax.axis_size(axis))
    route = [(i - distance, i) for i in devices if i - distance in devices]
    return lax.ppermute(block, axis, route)


def for_sending(shard):
    return jax.tree.map(lambda a: a.astype(jnp.bfloat16) if a.dtype == jnp.float32 else a, shard)


def lower_mask(length):
    return lax.broadcasted_iota(jnp.int32, (length, length), 0) >= lax.broadcasted_iota(
        jnp.int32, (length, length), 1
    )


def shard_output(q_float, k_float, v_float, cumulative, incoming):
    lower = lower_mask(q_float.shape[0])[None]
    gaps = cumulative[:, :, None] - cumulative[:, None, :]
    weights = jnp.where(lower, jnp.exp(jnp.where(lower, gaps, 0.0)), 0.0)
    scores = jnp.einsum("thd,uhd->htu", q_float, k_float, precision=exact_precision) * weights
    inner_part = jnp.einsum("htu,uhe->the", scores, v_float, precision=exact_precision)
    outer_part = jnp.einsum(
        "thd,hde->the",
        q_float * jnp.exp(cumulative).T[:, :, None],
        incoming,
        precision=exact_precision,
    )
    return inner_part + outer_part


def shard_state(k_float, v_float, cumulative):
    tail_decay = jnp.exp(cumulative[:, -1:] - cumulative)
    return jnp.einsum(
        "uhd,uhe->hde", k_float * tail_decay.T[:, :, None], v_float, precision=exact_precision
    )


def chain_join(earlier, later):
    return (earlier[0] * later[0], later[0][:, None, None] * earlier[1] + later[1])


def scores_work(query_two, keys_block, allowed, scale):
    raw_scores = (
        jnp.einsum("thd,uhd->htu", query_two, keys_block, preferred_element_type=jnp.float32)
        * scale
    )
    return jnp.where(allowed[None], raw_scores, floor_score)


def probs_work(tile_scores, log_mass, allowed, values_block):
    prob = jnp.where(allowed[None], jnp.exp(tile_scores - log_mass[:, :, None]), 0.0)
    part_out = jnp.einsum(
        "htu,uhd->thd", prob.astype(jnp.bfloat16), values_block, preferred_element_type=jnp.float32
    )
    return (prob, part_out)


def grads_work(prob, query_two, out_grad, keys_block, values_block, delta, scale):
    grad_prob = jnp.einsum(
        "thd,uhd->htu", out_grad, values_block, preferred_element_type=jnp.float32
    )
    grad_score = (prob * (grad_prob - delta.T[:, :, None]) * scale).astype(jnp.bfloat16)
    query_grad = jnp.einsum(
        "htu,uhd->thd", grad_score, keys_block, preferred_element_type=jnp.float32
    )
    key_grad = jnp.einsum("htu,thd->uhd", grad_score, query_two, preferred_element_type=jnp.float32)
    value_grad = jnp.einsum(
        "htu,thd->uhd", prob.astype(jnp.bfloat16), out_grad, preferred_element_type=jnp.float32
    )
    return (query_grad, key_grad, value_grad)


def ring_body(query_one, key_one, value_one, log_decay, query_two, key_two, out_grad, doc_ids):
    length, heads_here, width = query_one.shape
    shards = lax.axis_size("seq")
    token_position = lax.axis_index("seq")
    features = heads_here * lax.axis_size("head") * width
    q_float = query_one.astype(jnp.float32)
    k_float = key_one.astype(jnp.float32)
    v_float = value_one.astype(jnp.float32)
    cumulative = jnp.cumsum(log_decay, axis=1)
    carry_decay = jnp.exp(cumulative[:, -1])
    local_state, state_pull = jax.vjp(partial(shard_state, cumulative=cumulative), k_float, v_float)
    identity = (jnp.ones_like(carry_decay), jnp.zeros_like(local_state))
    incoming = prefix((carry_decay, local_state), "seq", chain_join, identity, False)[1]
    raw_out, output_pull = jax.vjp(
        partial(shard_output, cumulative=cumulative, incoming=incoming), q_float, k_float, v_float
    )
    square_sum = lax.psum(jnp.sum(raw_out * raw_out, axis=(1, 2)), "head")
    inverse = 1.0 / jnp.sqrt(square_sum / features + norm_epsilon)
    normed = raw_out * inverse[:, None, None]
    values_two = normed.astype(jnp.bfloat16)
    blocks_here = length // BLOCK
    scale = 1.0 / math.sqrt(width)
    offsets = jnp.arange(length, dtype=jnp.int32)
    query_doc = jnp.repeat(
        lax.dynamic_slice_in_dim(doc_ids, token_position * blocks_here, blocks_here), BLOCK
    )
    query_pos = token_position * length + offsets
    masks = []
    for distance in range(REACH + 1):
        source = (token_position - distance) % shards
        key_doc = jnp.repeat(
            lax.dynamic_slice_in_dim(doc_ids, source * blocks_here, blocks_here), BLOCK
        )
        key_pos = source * length + offsets
        masks.append(
            (key_pos[None, :] <= query_pos[:, None]) & (key_doc[None, :] == query_doc[:, None])
        )
    blocks = [(key_two, values_two)]
    current = (key_two, values_two)
    for distance in range(1, REACH + 1):
        current = from_behind((current[0], current[1]), "seq", 1)
        blocks.append(current)
    row_shape = (length, heads_here, width)
    peak_now = jnp.full((heads_here, length), floor_score, jnp.float32)
    mass_now = jnp.zeros((heads_here, length), jnp.float32)
    tile_list = []
    for distance in range(REACH + 1):
        allowed = masks[distance]
        tile_scores = scores_work(query_two, blocks[distance][0], allowed, scale)
        peak_next = jnp.maximum(peak_now, jnp.max(tile_scores, axis=2))
        fresh_mass = jnp.sum(
            jnp.where(allowed[None], jnp.exp(tile_scores - peak_next[:, :, None]), 0.0), axis=2
        )
        mass_now = mass_now * jnp.exp(peak_now - peak_next) + fresh_mass
        peak_now = peak_next
        tile_list.append(tile_scores)
    log_mass = peak_now + jnp.log(mass_now)
    attended = jnp.zeros(row_shape, jnp.float32)
    prob_list = []
    for distance in range(REACH + 1):
        allowed = masks[distance]
        prob, part_out = probs_work(tile_list[distance], log_mass, allowed, blocks[distance][1])
        attended = attended + part_out
        prob_list.append(prob)
    delta = jnp.sum(out_grad.astype(jnp.float32) * attended, axis=2)
    grad_query_two = jnp.zeros(row_shape, jnp.float32)
    carried = None
    for distance in range(REACH, -1, -1):
        keys_block, values_block = blocks[distance]
        query_grad, key_grad, value_grad = grads_work(
            prob_list[distance], query_two, out_grad, keys_block, values_block, delta, scale
        )
        grad_query_two = grad_query_two + query_grad
        if carried is None:
            carried = (key_grad, value_grad)
        else:
            moved = jax.tree.map(
                lambda part, own: part.astype(own.dtype),
                from_behind(for_sending(carried), "seq", -1),
                carried,
            )
            carried = (moved[0] + key_grad, moved[1] + value_grad)
    grad_key_two, grad_values_two = carried
    cross_sum = lax.psum(jnp.sum(raw_out * grad_values_two, axis=(1, 2)), "head")
    grad_raw = (
        inverse[:, None, None] * grad_values_two
        - raw_out * (inverse**3 * cross_sum / features)[:, None, None]
    )
    direct_state = jnp.einsum(
        "thd,the->hde",
        q_float * jnp.exp(cumulative).T[:, :, None],
        grad_raw,
        precision=exact_precision,
    )
    later_grad = prefix((carry_decay, direct_state), "seq", chain_join, identity, True)[1]
    grad_query_one, grad_key_out, grad_value_out = output_pull(grad_raw)
    grad_key_state, grad_value_state = state_pull(later_grad)
    return (
        grad_query_one,
        grad_key_out + grad_key_state,
        grad_value_out + grad_value_state,
        grad_query_two,
        grad_key_two,
    )


f32, bf16 = (jnp.float32, jnp.bfloat16)
LOG2E = math.log2(math.e)
PART_ROWS = 16


def dot(a, b):
    return lax.dot_general(a, b, (((1,), (0,)), ((), ())), preferred_element_type=f32)


def dot_nt(a, b):
    return lax.dot_general(a, b, (((1,), (1,)), ((), ())), preferred_element_type=f32)


def dot_tn(a, b):
    return lax.dot_general(a, b, (((0,), (0,)), ((), ())), preferred_element_type=f32)


def two_parts(value):
    high = value.astype(bf16)
    return high, (value - high.astype(f32)).astype(bf16)


def row_sums(value):
    ones = jnp.ones((PART_ROWS, value.shape[1]), bf16)
    high, low = two_parts(value)
    return dot_nt(ones, high) + dot_nt(ones, low)


def decay_column(parts):
    log_row = jnp.sum(parts.astype(f32), axis=0, keepdims=True)
    return jnp.sum(jnp.where(lower_mask(BLOCK), log_row, 0.0), axis=1, keepdims=True)


def chunk_decays(parts):
    lower = lower_mask(BLOCK)
    column = decay_column(parts)
    upper = lax.broadcasted_iota(jnp.int32, (BLOCK, BLOCK), 0) <= lax.broadcasted_iota(
        jnp.int32, (BLOCK, BLOCK), 1
    )
    row = jnp.sum(dot(parts, jnp.where(upper, 1.0, 0.0).astype(bf16)), axis=0, keepdims=True)
    last = column[BLOCK - 1 : BLOCK, :]
    weights = jnp.exp(jnp.where(lower, column - row, floor_score))
    return weights, jnp.exp(column), jnp.exp(last - column), jnp.exp(last)


def lightning_piece(ref, place):
    arrays = [ref[place, n * BLOCK : (n + 1) * BLOCK, :] for n in range(3)]
    return arrays + [chunk_decays(ref[place, ref.shape[1] - PART_ROWS :, :])]


UNROLL = 16


def over_chunks(chunks, body, carry, backward=False):
    unrolled = math.gcd(UNROLL, chunks)

    def step(n, carry):
        for part in range(unrolled):
            c = n * unrolled + part
            carry = body(chunks - 1 - c if backward else c, carry)
        return carry

    if unrolled == chunks:
        return step(0, carry)
    return lax.fori_loop(0, chunks // unrolled, step, carry)


def block_rows(c):
    if isinstance(c, int):
        return slice(c * BLOCK, (c + 1) * BLOCK)
    return pl.ds(pl.multiple_of(c * BLOCK, BLOCK), BLOCK)


def linear_state(heads, second_ref, state_ref):
    chunks, width = (second_ref.shape[0] // heads, second_ref.shape[2])

    def chunk(c, states):
        following = []
        for head in range(heads):
            _, k, v, (_, _, tail, whole) = lightning_piece(second_ref, c * heads + head)
            following.append(
                whole * states[head] + dot_tn(k, (v.astype(f32) * tail).astype(bf16))
            )
        return tuple(following)

    states = over_chunks(chunks, chunk, (jnp.zeros((width, width), f32),) * heads)
    for head in range(heads):
        state_ref[head] = states[head]


def value_gradient(half, kept_ref, other_ref, head, c):
    return jnp.where(
        half == head, kept_ref[block_rows(c), :], other_ref[block_rows(c), :].astype(f32)
    )


def linear_local(heads, second_ref, raw_ref):
    chunks, width = (second_ref.shape[0] // heads, second_ref.shape[2])

    def chunk(c, states):
        following = []
        for head in range(heads):
            q, k, v, (weights, grow, tail, whole) = lightning_piece(second_ref, c * heads + head)
            prob = (dot_nt(q, k) * weights).astype(bf16)
            raw = dot(prob, v) + grow * dot(q, states[head].astype(bf16))
            raw_ref[head, block_rows(c), :] = raw
            following.append(
                whole * states[head] + dot_tn(k, (v.astype(f32) * tail).astype(bf16))
            )
        return tuple(following)

    over_chunks(chunks, chunk, (jnp.zeros((width, width), f32),) * heads)


def linear_output(
    heads, info_ref, second_ref, incoming_ref, local_ref, kept_ref, other_ref, raw_ref, sent_ref, sums_ref
):
    chunks = second_ref.shape[0] // heads
    half = info_ref[info_ref.shape[0] - 1]
    incoming = [incoming_ref[head].astype(bf16) for head in range(heads)]
    carried = [jnp.ones((1, 1), f32)] * heads
    columns = jnp.zeros((BLOCK, BLOCK), f32)
    lanes = lax.broadcasted_iota(jnp.int32, (BLOCK, BLOCK), 1)
    for c in range(chunks):
        here = block_rows(c)
        raws = []
        squares, products = (0.0, 0.0)
        for head in range(heads):
            place = c * heads + head
            logs = decay_column(second_ref[place, second_ref.shape[1] - PART_ROWS :, :])
            outer = dot(second_ref[place, 0:BLOCK, :], incoming[head])
            raw = local_ref[head, here, :] + (carried[head] * jnp.exp(logs)) * outer
            carried[head] = carried[head] * jnp.exp(logs[BLOCK - 1 : BLOCK, :])
            grad = value_gradient(half, kept_ref, other_ref, head, c)
            squares = squares + raw * raw
            products = products + raw * grad
            raws.append(raw.astype(bf16))
            raw_ref[head, here, :] = raws[head]
        sent_ref[here, :] = jnp.where(half == 0, raws[1], raws[0])
        for place, part in ((c, squares), (chunks + c, products)):
            total = jnp.sum(part, axis=1, keepdims=True)
            columns = jnp.where(lanes == place, total, columns)
    sums_ref[...] = columns.T[0 : 2 * chunks, :]


def column(columns, c):
    if isinstance(c, int):
        return columns[:, c : c + 1]
    lanes = lax.broadcasted_iota(jnp.int32, columns.shape, 1)
    return jnp.sum(jnp.where(lanes == c, columns, 0.0), axis=1, keepdims=True)


def norm_columns(features, sums_ref):
    chunks = sums_ref.shape[0] // 2
    inverse = 1.0 / jnp.sqrt(sums_ref[0:chunks, :] / features + norm_epsilon)
    return inverse.T, (inverse * inverse * inverse * sums_ref[chunks:, :] / features).T


def linear_state_grad(
    features, heads, info_ref, second_ref, raw_ref, sums_ref, kept_ref, other_ref, state_grad_ref
):
    chunks, width = (second_ref.shape[0] // heads, second_ref.shape[2])
    half = info_ref[info_ref.shape[0] - 1]
    inverse, cross = norm_columns(features, sums_ref)

    def chunk(c, grads):
        following = []
        for head in range(heads):
            q, _, _, (_, grow, _, whole) = lightning_piece(second_ref, c * heads + head)
            grad = column(inverse, c) * value_gradient(half, kept_ref, other_ref, head, c)
            grad = grad - raw_ref[head, block_rows(c), :].astype(f32) * column(cross, c)
            following.append(whole * grads[head] + dot_tn(q, (grad * grow).astype(bf16)))
        return tuple(following)

    grads = over_chunks(chunks, chunk, (jnp.zeros((width, width), f32),) * heads, True)
    for head in range(heads):
        state_grad_ref[head] = grads[head]


def linear_backward(
    features, heads, info_ref, second_ref, raw_ref, incoming_ref, sums_ref, kept_ref, other_ref, later_ref,
    out_ref, state_s,
):
    chunks = second_ref.shape[0] // heads

    def before(c, states):
        following = []
        for head in range(heads):
            _, k, v, (_, _, tail, whole) = lightning_piece(second_ref, c * heads + head)
            state_s[head, c] = states[head].astype(bf16)
            following.append(
                whole * states[head] + dot_tn(k, (v.astype(f32) * tail).astype(bf16))
            )
        return tuple(following)

    over_chunks(chunks, before, tuple(incoming_ref[head] for head in range(heads)))
    half = info_ref[info_ref.shape[0] - 1]
    inverse, cross = norm_columns(features, sums_ref)

    def chunk(c, grads):
        following = []
        for head in range(heads):
            place = c * heads + head
            q, k, v, (weights, grow, tail, whole) = lightning_piece(second_ref, place)
            grad = column(inverse, c) * value_gradient(half, kept_ref, other_ref, head, c)
            grad = grad - raw_ref[head, block_rows(c), :].astype(f32) * column(cross, c)
            grad_low = grad.astype(bf16)
            prob = (dot_nt(q, k) * weights).astype(bf16)
            grad_score = (dot_nt(grad_low, v) * weights).astype(bf16)
            state_low = grads[head].astype(bf16)
            query_grad = dot(grad_score, k) + grow * dot_nt(grad_low, state_s[head, c])
            key_grad = dot_tn(grad_score, q) + tail * dot_nt(v, state_low)
            value_grad = dot_tn(prob, grad_low) + tail * dot(k, state_low)
            following.append(whole * grads[head] + dot_tn(q, (grad * grow).astype(bf16)))
            out_ref[place, 0:BLOCK, :] = query_grad.astype(bf16)
            out_ref[place, BLOCK : 2 * BLOCK, :] = key_grad.astype(bf16)
            out_ref[place, 2 * BLOCK : 3 * BLOCK, :] = value_grad.astype(bf16)
        return tuple(following)

    over_chunks(chunks, chunk, tuple(later_ref[head] for head in range(heads)), True)


TOGETHER = 4
GROUP = TOGETHER * BLOCK


def by_window(info_ref, chunks, window):
    def step(group, carry):
        end = TOGETHER * (group + 1)
        need = end - info_ref[TOGETHER * group]
        least = 0
        for blocks in window_sizes(chunks):
            begin = end - blocks
            pl.when((need > least) & (need <= blocks))(partial(window, group, begin, blocks))
            least = blocks
        return carry

    lax.fori_loop(0, chunks // TOGETHER, step, 0)


def window_sizes(chunks):
    return range(TOGETHER, min(chunks, REACH + TOGETHER) + 1, 2)


def window_scores(info_ref, keys, queries, group, begin):
    shape = (keys.shape[0], queries.shape[0])
    scores = dot(keys, queries.T) * (LOG2E / math.sqrt(keys.shape[1]))
    u_pos = begin + lax.broadcasted_iota(jnp.int32, shape, 0)
    lane = lax.broadcasted_iota(jnp.int32, (1, shape[1]), 1)
    lowest = jnp.zeros_like(lane)
    for n in range(TOGETHER):
        lowest = jnp.where(lane >= n * BLOCK, info_ref[TOGETHER * group + n] * BLOCK, lowest)
    return scores, (u_pos >= lowest) & (u_pos <= group * GROUP + lane)


def blocks_of(first_ref, place, block, count):
    rows = first_ref[pl.ds(block, count), place * BLOCK : (place + 1) * BLOCK, :]
    return rows.reshape(count * BLOCK, first_ref.shape[2])


def softmax_masses(info_ref, first_ref, mass_ref, kept_ref, sent_ref, value_grad_s):
    chunks, width = (first_ref.shape[0], first_ref.shape[2])
    value_grad_s[...] = jnp.zeros_like(value_grad_s)

    def window(group, begin, blocks):
        rows = pl.ds(pl.multiple_of(begin * BLOCK, 2 * BLOCK), blocks * BLOCK)
        scores, allowed = window_scores(
            info_ref,
            blocks_of(first_ref, 1, begin, blocks),
            blocks_of(first_ref, 0, TOGETHER * group, TOGETHER),
            group,
            begin * BLOCK,
        )
        scores = jnp.where(allowed, scores, floor_score)
        peak = jnp.max(scores, axis=0, keepdims=True)
        mass = jnp.exp2(scores - peak)
        total = jnp.sum(mass, axis=0, keepdims=True)
        mass_ref[pl.ds(group, 1), :] = peak + jnp.log2(total)
        prob = (mass * (1.0 / total)).astype(bf16)
        value_grad_s[rows, :] += dot(prob, blocks_of(first_ref, 2, TOGETHER * group, TOGETHER))

    by_window(info_ref, chunks, window)
    half = info_ref[info_ref.shape[0] - 1]
    for c in range(chunks // 2):
        low = value_grad_s[block_rows(c), :]
        high = value_grad_s[block_rows(chunks // 2 + c), :]
        kept_ref[block_rows(c), :] = jnp.where(half == 0, low, high)
        sent_ref[block_rows(c), :] = jnp.where(half == 0, high, low).astype(bf16)


def softmax_grads(
    features, info_ref, first_ref, mass_ref, raw_ref, other_ref, sums_ref, other_sums_ref, out_ref,
    key_t_s, value_s, value_t_s, key_grad_s,
):
    chunks, width = (first_ref.shape[0], first_ref.shape[2])
    side = chunks // 2
    scale = 1.0 / math.sqrt(width)
    half = info_ref[info_ref.shape[0] - 1]
    inverse, other_inverse = [
        (1.0 / jnp.sqrt(ref[0:side, :] / features + norm_epsilon)).T for ref in (sums_ref, other_sums_ref)
    ]
    for c in range(chunks):
        here = block_rows(c)
        there = block_rows(c % side)
        own = jnp.where(half == 0, raw_ref[0, there, :], raw_ref[1, there, :])
        own = own.astype(f32) * column(inverse, c % side)
        other = other_ref[there, :].astype(f32) * column(other_inverse, c % side)
        v = jnp.where(half == c // side, own, other).astype(bf16)
        value_s[here, :] = v
        value_t_s[:, here] = v.T
        key_t_s[:, here] = first_ref[c, BLOCK : 2 * BLOCK, :].T
        key_grad_s[here, :] = jnp.zeros((BLOCK, width), f32)

    def window(group, begin, blocks):
        rows = pl.ds(pl.multiple_of(begin * BLOCK, 2 * BLOCK), blocks * BLOCK)
        queries = blocks_of(first_ref, 0, TOGETHER * group, TOGETHER)
        keys = blocks_of(first_ref, 1, begin, blocks)
        scores, allowed = window_scores(info_ref, keys, queries, group, begin * BLOCK)
        scores = jnp.where(allowed, scores - mass_ref[pl.ds(group, 1), :], floor_score)
        prob = jnp.exp2(scores)
        g_t = blocks_of(first_ref, 2, TOGETHER * group, TOGETHER).T
        attended = dot(value_t_s[:, rows], prob.astype(bf16))
        delta = jnp.sum(g_t.astype(f32) * attended, axis=0, keepdims=True)
        grad_prob = dot(value_s[rows, :], g_t)
        grad_score = (prob * ((grad_prob - delta) * scale)).astype(bf16)
        key_grad_s[rows, :] += dot(grad_score, queries)
        query_grad = dot(key_t_s[:, rows], grad_score).T.astype(bf16)
        for c in range(TOGETHER):
            out_ref[TOGETHER * group + c, 0:BLOCK, :] = query_grad[block_rows(c), :]

    by_window(info_ref, chunks, window)
    for c in range(chunks):
        out_ref[c, BLOCK : 2 * BLOCK, :] = key_grad_s[block_rows(c), :].astype(bf16)


def call(kernel, micros, outs, scratch, *operands, prefetch=0, room=8, whole=False):
    vmem = pl.BlockSpec(memory_space=pltpu.VMEM)
    smem = pl.BlockSpec(memory_space=pltpu.SMEM)
    results = [jax.ShapeDtypeStruct(shape, kind) for shape, kind in outs]
    held = [jax.ShapeDtypeStruct(shape, kind) for shape, kind in scratch]
    size = sum(
        a.size * a.dtype.itemsize for a in [*held, *(([*operands, *results]) if whole else [])]
    )
    return pl.pallas_call(
        kernel,
        out_shape=results,
        in_specs=[smem] * prefetch + [vmem] * (len(operands) - prefetch),
        out_specs=[vmem] * len(outs),
        scratch_shapes=[pltpu.VMEM(shape, kind) for shape, kind in scratch],
        compiler_params=pltpu.CompilerParams(vmem_limit_bytes=size + room * 1024 * 1024),
        cost_estimate=pl.CostEstimate(
            flops=int(micros * 1e9), bytes_accessed=int(micros * 3e6), transcendentals=0
        ),
    )(*operands)


def swap_matrix(chunks):
    size = chunks * chunks
    i = lax.broadcasted_iota(jnp.int32, (size, size), 0)
    j = lax.broadcasted_iota(jnp.int32, (size, size), 1)
    return jnp.where(j == (i % chunks) * chunks + i // chunks, 1.0, 0.0).astype(bf16)


def pair_order(heads):
    return [(h % 2) * (heads // 2) + h // 2 for h in range(heads)]


def pack(order, *refs):
    arrays, out_ref = ([ref for ref in refs[:-1] if len(ref.shape) == 3], refs[-1])
    length, heads, width = arrays[0].shape
    swap = swap_matrix(heads)
    for place, ref in enumerate(arrays):
        for begin in range(0, length, heads):
            rows = ref[begin : begin + heads].reshape(heads * heads, width)
            swapped = dot(swap, rows).astype(bf16)
            row = place * length + begin
            for h in range(heads):
                out_ref[order[h], row : row + heads, :] = swapped[h * heads : (h + 1) * heads, :]
    if len(arrays) == len(refs) - 1:
        return
    decay_ref = refs[-2]
    high, _ = two_parts(decay_ref[...])
    middle, last = two_parts(decay_ref[...] - high.astype(f32))
    row = lax.broadcasted_iota(jnp.int32, (PART_ROWS, length), 0)
    for h in range(heads):
        tile = jnp.zeros((PART_ROWS, length), f32)
        for n, part in enumerate((high, middle, last)):
            tile = jnp.where(row == n, part[h : h + 1, :].astype(f32), tile)
        out_ref[order[h], len(arrays) * length :, :] = tile.astype(bf16)


def unpack(order, in_ref, *outs):
    length, heads, width = outs[0].shape
    swap = swap_matrix(heads)
    for place, out_ref in enumerate(outs):
        for begin in range(0, length, heads):
            row = place * length + begin
            rows = jnp.concatenate(
                [in_ref[order[h], row : row + heads, :] for h in range(heads)], axis=0
            )
            out_ref[begin : begin + heads] = dot(swap, rows).reshape(heads, heads, width)


PIECES = 2


def streamed_pack(order, arrays):
    length, heads, width = arrays[0].shape
    part = length // PIECES

    def kernel(*refs):
        swap = swap_matrix(heads)
        out_ref = refs[-1]
        for place, ref in enumerate(refs[:-1]):
            for begin in range(0, part, heads):
                rows = ref[begin : begin + heads].reshape(heads * heads, width)
                swapped = dot(swap, rows).astype(bf16)
                for h in range(heads):
                    out_ref[order[h], place, begin : begin + heads, :] = swapped[
                        h * heads : (h + 1) * heads, :
                    ]

    packed = pl.pallas_call(
        kernel,
        grid=(PIECES,),
        out_shape=jax.ShapeDtypeStruct((heads, len(arrays), length, width), bf16),
        in_specs=[pl.BlockSpec((part, heads, width), lambda n: (n, 0, 0))] * len(arrays),
        out_specs=pl.BlockSpec((heads, len(arrays), part, width), lambda n: (0, 0, n, 0)),
        compiler_params=pltpu.CompilerParams(vmem_limit_bytes=16 * 1024 * 1024),
    )(*[pltpu.with_memory_space_constraint(array, pltpu.HBM) for array in arrays])
    return packed.reshape(heads, len(arrays) * length, width)


def exchange(x):
    return lax.all_to_all(x, "seq", 0, 0, tiled=True)


def exchange_half(x):
    side = lax.axis_size("seq") // 2
    groups = [list(range(side)), list(range(side, 2 * side))]
    return lax.all_to_all(x, "seq", 0, 0, tiled=True, axis_index_groups=groups)


def upward(x):
    side = lax.axis_size("seq") // 2
    return lax.ppermute(x, "seq", [(i, i + side) for i in range(side)])


def downward(x):
    side = lax.axis_size("seq") // 2
    return lax.ppermute(x, "seq", [(i + side, i) for i in range(side)])


def swapped(x):
    side = lax.axis_size("seq") // 2
    return lax.ppermute(x, "seq", [(i, (i + side) % (2 * side)) for i in range(2 * side)])


def over_heads(mine):
    count = lax.axis_size("head")
    total = mine
    for step in range(1, count):
        total = total + lax.ppermute(mine, "head", [(i, (i + step) % count) for i in range(count)])
    return total


def body(query_one, key_one, value_one, log_decay, query_two, key_two, out_grad, doc_ids):
    length, heads_here, width = query_one.shape
    shards = lax.axis_size("seq")
    if heads_here != shards or length != BLOCK or shards != 16 or width != BLOCK:
        return ring_body(
            query_one, key_one, value_one, log_decay, query_two, key_two, out_grad, doc_ids
        )
    side = shards // 2
    heads = heads_here // side
    half_length = side * length
    features = heads_here * lax.axis_size("head") * width
    half = (lax.axis_index("seq") >= side).astype(jnp.int32)
    starts = jnp.sum((doc_ids[None, :] < doc_ids[:, None]).astype(jnp.int32), axis=1)
    info = jnp.concatenate([starts, half[None]])
    straight, paired = (list(range(heads_here)), pair_order(heads_here))

    def packed(order, rows, arrays, *more):
        arrays = [pltpu.with_memory_space_constraint(array, pltpu.HBM) for array in arrays]
        return call(
            partial(pack, order), 3, [((heads_here, rows, width), bf16)], [], *arrays, *more, whole=True
        )[0]

    first = exchange(streamed_pack(paired, (query_two, key_two, out_grad)))
    second = packed(straight, 3 * length + PART_ROWS, (query_one, key_one, value_one), log_decay)
    second, first = lax.optimization_barrier((second, first))
    second = exchange_half(second)
    half_rows = (half_length, width)
    full_rows = (shards * length, width)
    masses, grad_kept, grad_sent = call(
        softmax_masses,
        6,
        [
            ((shards // TOGETHER, GROUP), f32),
            (half_rows, f32),
            (half_rows, bf16),
        ],
        [(full_rows, f32)],
        info,
        first,
        prefetch=1,
    )
    grad_other = swapped(grad_sent)
    state_shape = (heads, width, width)
    (state,) = call(partial(linear_state, heads), 1, [(state_shape, f32)], [], second)
    incoming = upward(state)
    head_rows = (heads, half_length, width)
    (local,) = call(partial(linear_local, heads), 4, [(head_rows, f32)], [], second)
    raw, raw_sent, sums = call(
        partial(linear_output, heads),
        2,
        [(head_rows, bf16), (half_rows, bf16), ((2 * side, BLOCK), f32)],
        [],
        info,
        second,
        incoming,
        local,
        grad_kept,
        grad_other,
        prefetch=1,
    )
    raw_other = swapped(raw_sent)
    sums = exchange_half(jnp.broadcast_to(sums[None], (side,) + sums.shape))
    sums = over_heads(jnp.sum(sums, axis=0))
    sums_other = swapped(sums[:side])
    (softmax_grad,) = call(
        partial(softmax_grads, features),
        7,
        [((shards, 2 * BLOCK, width), bf16)],
        [
            ((width, shards * length), bf16),
            (full_rows, bf16),
            ((width, shards * length), bf16),
            (full_rows, f32),
        ],
        info,
        first,
        masses,
        raw,
        raw_other,
        sums,
        sums_other,
        prefetch=1,
    )
    raw_in_hbm = pltpu.with_memory_space_constraint(raw, pltpu.HBM)
    other_in_hbm = pltpu.with_memory_space_constraint(grad_other, pltpu.HBM)
    kept_in_hbm = pltpu.with_memory_space_constraint(grad_kept, pltpu.HBM)
    (state_grad,) = call(
        partial(linear_state_grad, features, heads),
        2,
        [(state_shape, f32)],
        [],
        info,
        second,
        raw_in_hbm,
        sums,
        kept_in_hbm,
        other_in_hbm,
        prefetch=1,
    )
    later_grad = downward(state_grad)
    later_grad, softmax_grad = lax.optimization_barrier((later_grad, softmax_grad))
    softmax_grad = exchange(softmax_grad)
    (linear_grads,) = call(
        partial(linear_backward, features, heads),
        5,
        [((heads_here, 3 * BLOCK, width), bf16)],
        [((heads, side, width, width), bf16)],
        info,
        second,
        raw_in_hbm,
        incoming,
        sums,
        kept_in_hbm,
        other_in_hbm,
        later_grad,
        prefetch=1,
    )
    softmax_grad, linear_grads = lax.optimization_barrier((softmax_grad, linear_grads))
    linear_grads = exchange_half(linear_grads)

    def unpacked(order, count, received):
        outs = [((length, heads_here, width), f32)] * count
        return call(partial(unpack, order), count, outs, [], received, whole=True)

    query_one_grad, key_one_grad, value_one_grad = unpacked(straight, 3, linear_grads)
    query_two_grad, key_two_grad = unpacked(paired, 2, softmax_grad)
    return (query_one_grad, key_one_grad, value_one_grad, query_two_grad, key_two_grad)


def solution(mesh):
    placed = (
        P("seq", "head", None),
        P("seq", "head", None),
        P("seq", "head", None),
        P("head", "seq"),
        P("seq", "head", None),
        P("seq", "head", None),
        P("seq", "head", None),
        P(),
    )
    return jax.shard_map(
        body,
        mesh=mesh,
        in_specs=placed,
        out_specs=(P("seq", "head", None),) * 5,
        check_vma=False,
    )
```
